32 devices in a mesh: gx: 4 (over z), gy: 4 (over y, x), blk: 2 (over core).
Axes of the slice: x: 2, y: 2, z: 4, core: 2. Of those that a mesh axis runs over, the one named last changes fastest.
Arguments:
- pressure: float32 [64, 256, 256], P('gx', 'gy', 'blk'), may hold values from -6 to 6
- pressure_prev: float32 [64, 256, 256], P('gx', 'gy', 'blk'), may hold values from -6 to 6
- buoyancy: float32 [64, 256, 256], P('gx', 'gy', 'blk'), may hold values from 0.5 to 2
- kappa: float32 [64, 256, 256], P('gx', 'gy', 'blk'), may hold values from 0.5 to 2
- hull_accel: float32 [16384, 128], P(('gx', 'gy', 'blk')), may hold values from -6 to 6
- row_block: int32 [16384, 1], P(('gx', 'gy', 'blk')), may hold values from 0 to 15; in each aligned block of 512 rows (0 to 511, 512 to 1023, ...) at most 64 rows name the same one
- row_column: int32 [16384, 1], P(('gx', 'gy', 'blk')), may hold values from 0 to 1023
Outputs:
- pressure_next: float32 [64, 256, 256], P('gx', 'gy', 'blk')
- hull_pressure: float32 [16384, 128], P(('gx', 'gy', 'blk'))
The draws below stay inside these ranges and needn't reach their ends.
Inputs may be any that keep to these rules, and one draw needn't show every extreme that they name: `row_block`: among the 512 rows of one device at most 64 name the same block, and exactly 64 do for some block.
All inputs are finite; a program needn't handle non-finite values.
Results may differ from the reference program's by a relative error of at most 0.00002.
Values sent between devices are 32-bit elements; how exact they have to be, the bound alone decides.
No kernel may reach another device: no remote copies, remote signals or barrier semaphores. Data moves between devices by JAX's collectives and lax.ppermute only.
A program may use at most 64 MiB of HBM per device.

```python
import math
import jax
import jax.numpy as jnp
import numpy as np
from jax import lax

CX = 16
CY = 64
CZ = 128
HROWS = 512
NX = 64
NY = 256
NZ = 256
CAP = 64
HULL = 16384
N_GX = 4
N_GY = 4
N_BLK = 2


def set_ends(entries, key, least, largest):
    spot = [jax.random.randint(jax.random.fold_in(key, axis), (), 0, length) for axis, length in enumerate(entries.shape)]
    longest = entries.shape.index(max(entries.shape))
    neighbour = spot[:longest] + [(spot[longest] + 1) % entries.shape[longest]] + spot[longest + 1:]
    return entries.at[tuple(spot)].set(least).at[tuple(neighbour)].set(largest)


def levels(key, dims, shards, least, largest):
    level, own = 1.0, jax.random.fold_in(key, 6)
    for axis_at, blocks in shards:
        heights = jnp.exp(jax.random.uniform(jax.random.fold_in(own, axis_at), (blocks,), jnp.float32, least / len(shards), largest / len(shards)))
        level = level * jnp.repeat(heights, dims[axis_at] // blocks).reshape([-1 if axis == axis_at else 1 for axis in range(len(dims))])
    return level


def assign_block(stream_key, own, number, rows, count, top, reach, slope):
    sequence = jax.random.permutation(stream_key, count)
    packed, common = portions_of(count, rows * top, reach, slope, True), portions_of(count, rows * top, reach, slope, False)
    places = jnp.arange(count)

    def named(lengths, rotation):
        used = int((lengths > 0).sum())
        fixed = max(1, used // 4)
        moved = fixed + (places - fixed + rotation * (used - fixed)) % max(1, count - fixed)
        return jnp.zeros((count,), jnp.int32).at[sequence[jnp.where(places < fixed, places, moved)]].set(jnp.asarray(lengths, jnp.int32))

    lengths = jnp.where(number % 4 == 0, named(packed, number // 4), named(common, number - number // 4 - 1))
    mixed = jax.random.permutation(jax.random.fold_in(own, 3), count)
    giver, receiver = mixed[0:count // 2 * 2:2], mixed[1:count // 2 * 2:2]
    room = jnp.minimum(lengths[giver] - 1, reach - lengths[receiver]) // 2
    room = jnp.where((giver == sequence[0]) | (receiver == sequence[0]) | (lengths[receiver] == 0), 0, jnp.maximum(room, 0))
    moved = jax.random.randint(jax.random.fold_in(own, 4), (count // 2,), 0, 1 << 20) % (room + 1)
    lengths = lengths.at[giver].add(-moved).at[receiver].add(moved)
    items = jnp.searchsorted(jnp.cumsum(lengths), jnp.arange(rows * top), side="right").astype(jnp.int32)
    listing = items.reshape(top, rows).T
    listing = listing[jax.random.permutation(jax.random.fold_in(own, 1), rows)]
    rotation = jax.random.randint(jax.random.fold_in(own, 2), (rows, 1), 0, top)
    return jnp.take_along_axis(listing, (jnp.arange(top)[None, :] + rotation) % top, axis=1)


def portions_of(count, total, most, skew, full):
    portions = [(1 << 20) // math.isqrt(grade ** skew) + 1 for grade in range(1, count + 1)]
    largest = most if full else min(most, max(-(-total // count), total * portions[0] // sum(portions)))
    least = 1 if total - largest >= count - 1 else 0
    holding, spare = [largest] + [least] * (count - 1), total - largest - least * (count - 1)
    while spare > 0:
        movable = [i for i in range(1, count) if holding[i] < largest] or [i for i in range(1, count) if holding[i] < most]
        mass, remaining = sum([portions[i] for i in movable]), spare
        for i in movable:
            more = min(most - holding[i], max(1, remaining * portions[i] // mass), spare)
            holding[i] = holding[i] + more
            spare = spare - more
    return np.array(holding)


def scatter_about(own_key, extent, scale, reach, shards=(), held_as=jnp.bfloat16):
    loudness = levels(own_key, extent, shards, -0.22, 0.18) if shards else 1.0
    entries = jax.random.normal(own_key, extent, jnp.float32) * scale * loudness
    return jnp.minimum(jnp.maximum(entries, -reach), reach).astype(held_as)


def setup_inputs(seed: int = 0) -> dict:
    key_of = jax.random.split(jax.random.key(seed), 8)
    pressure = scatter_about(key_of[0], (NX, NY, NZ), 1.0, 6.0, ((0, 4), (1, 4), (2, 2)), jnp.float32)
    pressure_prev = scatter_about(key_of[1], (NX, NY, NZ), 1.0, 6.0, ((0, 4), (1, 4), (2, 2)), jnp.float32)
    buoyancy = jnp.clip(jnp.exp(math.log(2.0) - 1.3862944 * jax.random.uniform(key_of[2], (NX, NY, NZ), jnp.float32) ** levels(key_of[2], (NX, NY, NZ), ((0, 4), (1, 4), (2, 2)), -0.2, 0.2)), 0.5, 2.0)
    kappa = jnp.clip(jnp.exp(math.log(2.0) - 1.3862944 * jax.random.uniform(key_of[3], (NX, NY, NZ), jnp.float32) ** levels(key_of[3], (NX, NY, NZ), ((0, 4), (1, 4), (2, 2)), -0.2, 0.2)), 0.5, 2.0)
    hull_accel = scatter_about(key_of[4], (HULL, CZ), 1.0, 6.0, ((0, 32),), jnp.float32)
    row_block_keys = jax.random.split(jax.random.fold_in(key_of[5], 1), HULL // HROWS)
    row_block_turns = jax.random.permutation(jax.random.fold_in(key_of[5], 3), HULL // HROWS)
    row_block = jax.vmap(lambda own, number: assign_block(jax.random.fold_in(key_of[5], 2), own, number, HROWS, N_GX * N_GY, 1, CAP, 2))(row_block_keys, row_block_turns).reshape((HULL, 1))
    row_column = set_ends(jax.random.randint(key_of[6], (HULL, 1), 0, CX * CY), jax.random.fold_in(key_of[6], 1), 0, (CX * CY) - 1).astype(jnp.int32)
    return dict(pressure=pressure, pressure_prev=pressure_prev, buoyancy=buoyancy, kappa=kappa, hull_accel=hull_accel, row_block=row_block, row_column=row_column)


courant_sq = 0.05
source_gain = 0.5


def trim_edge(field, width, skip_dim):
    for other_dim in range(3):
        if other_dim != skip_dim:
            field = lax.slice_in_dim(field, width, field.shape[other_dim] - width, axis=other_dim)
    return field


def fourth_diff(field, along_dim, length_out):
    def shifted(offset):
        return lax.slice_in_dim(field, offset, offset + length_out, axis=along_dim)
    return (27.0 * (shifted(2) - shifted(1)) - (shifted(3) - shifted(0))) / 24.0


def operator(padded, buoy_pad):
    summed = None
    for along_dim in range(3):
        press_line = trim_edge(padded, 3, along_dim)
        buoy_line = trim_edge(buoy_pad, 2, along_dim)
        length_out = padded.shape[along_dim] - 6
        gradient = fourth_diff(press_line, along_dim, length_out + 3)
        face_buoy = (lax.slice_in_dim(buoy_line, 0, length_out + 3, axis=along_dim)
                     + lax.slice_in_dim(buoy_line, 1, length_out + 4, axis=along_dim)) * 0.5
        axis_term = fourth_diff(gradient * face_buoy, along_dim, length_out)
        summed = axis_term if summed is None else summed + axis_term
    return summed


def reference(pressure, pressure_prev, buoyancy, kappa, hull_accel, row_block, row_column):
    hull_rows = hull_accel.shape[0]
    device_ids = jnp.arange(hull_rows, dtype=jnp.int32) // HROWS
    depth = (device_ids % N_BLK).astype(jnp.int32)
    block_ids = row_block[:, 0].astype(jnp.int32)
    column = row_column[:, 0].astype(jnp.int32)
    x_cells = (block_ids // N_GY) * CX + column // CY
    y_cells = (block_ids % N_GY) * CY + column % CY
    source = jnp.zeros((NX, NY, N_BLK, CZ), jnp.float32).at[x_cells, y_cells, depth].add(hull_accel)
    source = source.reshape(NX, NY, NZ)
    buoy_pad = jnp.pad(buoyancy, 2)
    lap_one = operator(jnp.pad(pressure, 3), buoy_pad)
    pressure_mid = 2.0 * pressure - pressure_prev + kappa * (courant_sq * lap_one + source_gain * source)
    lap_two = operator(jnp.pad(pressure_mid, 3), buoy_pad)
    pressure_next = 2.0 * pressure_mid - pressure + kappa * (courant_sq * lap_two + source_gain * source)
    picked = pressure_next.reshape(NX, NY, N_BLK, CZ)[x_cells, y_cells, depth]
    return pressure_next, picked
```

```python
import functools

import jax
import jax.numpy as jnp
from jax import lax
from jax.experimental import pallas as pl
from jax.experimental.pallas import tpu as pltpu
from jax.sharding import PartitionSpec as P

courant_sq = 0.05
source_gain = 0.5
lap_scale = courant_sq * 0.5 / (24.0 * 24.0)
halo = 3
tile = 8
f32 = jnp.float32
bf16 = jnp.bfloat16
VMEM_LIMIT = 16 << 20


def run(kernel, outs, *args, flops=0, scratch=()):
    size = sum(4 * a.size for a in args) + sum(4 * o.size for o in outs)
    spec = pl.BlockSpec(memory_space=pltpu.VMEM)
    return pl.pallas_call(
        kernel,
        out_shape=outs,
        in_specs=[spec] * len(args),
        out_specs=[spec] * len(outs),
        scratch_shapes=scratch,
        compiler_params=pltpu.CompilerParams(vmem_limit_bytes=VMEM_LIMIT),
        cost_estimate=pl.CostEstimate(flops=flops, bytes_accessed=size, transcendentals=0),
    )(*args)


def shaped(*shape, dtype=f32):
    return jax.ShapeDtypeStruct(shape, dtype)


def dot(a, b, contract=((1,), (0,))):
    return lax.dot_general(a, b, (contract, ((), ())), preferred_element_type=f32)


def parts_of(x):
    high = x.astype(bf16)
    rest = x - high.astype(f32)
    middle = rest.astype(bf16)
    low = (rest - middle.astype(f32)).astype(bf16)
    return jnp.concatenate([high, middle, low], axis=1)


def select_rows(one_hot, x):
    lanes = x.shape[1]
    y = dot(one_hot, parts_of(x))
    return y[:, :lanes] + y[:, lanes : 2 * lanes] + y[:, 2 * lanes :]


def one_hot_of(index, shape, dim):
    return jnp.where(lax.broadcasted_iota(jnp.int32, shape, dim) == index, 1.0, 0.0).astype(bf16)


def as_column(row):
    n = row.shape[1]
    diagonal = lax.broadcasted_iota(jnp.int32, (n, n), 0) == lax.broadcasted_iota(jnp.int32, (n, n), 1)
    return jnp.sum(jnp.where(diagonal, row, 0.0), axis=1, keepdims=True)


def pack_kernel(groups, cap, block_ref, column_ref, accel_ref, out_ref, place_ref):
    rows, lanes = accel_ref.shape
    stride = cap + tile
    block = block_ref[...]
    column = column_ref[...] + 1
    named = lax.broadcasted_iota(jnp.int32, (groups, rows), 0) == block
    matches = jnp.where(named, 1.0, 0.0).astype(bf16)
    before = lax.broadcasted_iota(jnp.int32, (rows, rows), 0) < lax.broadcasted_iota(jnp.int32, (rows, rows), 1)
    earlier = dot(matches, jnp.where(before, 1.0, 0.0).astype(bf16))
    slot = jnp.sum(jnp.where(named, earlier, 0.0), axis=0, keepdims=True).astype(jnp.int32)
    place_ref[...] = (block * cap + slot).astype(f32)
    out_ref[...] = select_rows(one_hot_of(block * stride + slot, (groups * stride, rows), 0), accel_ref[...])
    at_slot = lax.broadcasted_iota(jnp.int32, (lanes, rows), 0) % cap == slot
    high = jnp.where(at_slot, column // 32, 0).astype(f32).astype(bf16)
    low = jnp.where(at_slot, column % 32, 0).astype(f32).astype(bf16)
    columns = dot(matches, high, ((1,), (1,))) * 32.0 + dot(matches, low, ((1,), (1,)))
    for g in range(groups):
        out_ref[g * stride + cap : (g + 1) * stride, :] = jnp.broadcast_to(columns[g : g + 1], (tile, lanes))


def column_rows(got_ref, cap):
    groups, _, lanes = got_ref.shape
    per = lanes // cap
    lane = lax.broadcasted_iota(jnp.int32, (1, lanes), 1) // cap
    rows = []
    for g in range(0, groups, per):
        row = got_ref[g, cap : cap + 1, :]
        for k in range(1, per):
            row = jnp.where(lane == k, got_ref[g + k, cap : cap + 1, :], row)
        rows.append(row - 1.0)
    return rows


def mid_kernel(cap, got_ref, mid0_ref, kappa_ref, mid_ref, xe_ref, xo_ref, ye_ref, yo_ref, spread_ref):
    groups, _, lanes = got_ref.shape
    cx, cy, cz = mid0_ref.shape
    for at, row in enumerate(column_rows(got_ref, cap)):
        spread_ref[:, at * lanes : (at + 1) * lanes] = one_hot_of(row.astype(jnp.int32), (cx * cy, lanes), 0)
    rows = got_ref[:, :cap, :].reshape(groups * cap, lanes)
    source = select_rows(spread_ref[...], rows).reshape(cx, cy, cz)
    mid_ref[...] = mid0_ref[...] + kappa_ref[...] * (source_gain * source)
    send_faces(mid_ref, halo, xe_ref, xo_ref, ye_ref, yo_ref)


def gather_map_kernel(cap, cols, got_ref, map_ref):
    lanes = got_ref.shape[2]
    for at, row in enumerate(column_rows(got_ref, cap)):
        column = as_column(row).astype(jnp.int32)
        map_ref[at * lanes : (at + 1) * lanes, :] = one_hot_of(column, (lanes, cols), 1)


def unpack_map_kernel(lanes, place_ref, map_ref):
    rows, slots = map_ref.shape
    for at in range(0, rows, lanes):
        column = as_column(place_ref[:, at : at + lanes]).astype(jnp.int32)
        map_ref[at : at + lanes, :] = one_hot_of(column, (lanes, slots), 1)


def unpack_kernel(map_ref, returned_ref, out_ref):
    slots = map_ref.shape[1]
    out_ref[...] = select_rows(map_ref[...], returned_ref[...].reshape(slots, -1))


def start_of(axis, low, high, even_takes_high):
    even = lax.axis_index(axis) % 2 == 0
    return jnp.where(even, high, low) if even_takes_high else jnp.where(even, low, high)


def send_faces(ref, width, xe_ref, xo_ref, ye_ref, yo_ref):
    cx, cy, _ = ref.shape
    xe_ref[...] = ref[pl.ds(start_of("gx", 0, cx - width, True), width)]
    xo_ref[...] = ref[pl.ds(start_of("gx", 0, cx - width, False), width)]
    ye_ref[...] = ref[:, pl.ds(pl.multiple_of(start_of("gy", 0, cy - tile, True), tile), tile), :]
    yo_ref[...] = ref[:, pl.ds(pl.multiple_of(start_of("gy", 0, cy - tile, False), tile), tile), :]


def low_and_high(axis, from_even, from_odd):
    at = lax.axis_index(axis)
    even = at % 2 == 0
    low = jnp.where(at > 0, jnp.where(even, from_odd, from_even), 0.0)
    high = jnp.where(at < lax.axis_size(axis) - 1, jnp.where(even, from_even, from_odd), 0.0)
    return low, high


def swap_pairs(sizes, axis, first):
    num_gx, num_gy, num_blk = sizes
    pairs = []
    for x in range(num_gx):
        for y in range(num_gy):
            for b in range(num_blk):
                at, count = (x, num_gx) if axis == "gx" else (y, num_gy)
                other = at + 1 if at % 2 == first else at - 1
                if 0 <= other < count:
                    to = (other, y, b) if axis == "gx" else (x, other, b)
                else:
                    to = (x, y, num_blk - 1 - b)
                pairs.append(((x * num_gy + y) * num_blk + b, (to[0] * num_gy + to[1]) * num_blk + to[2]))
    return pairs


def exchange(xe, xo, ye, yo):
    axes = ("gx", "gy", "blk")
    sizes = tuple(lax.axis_size(a) for a in axes)
    return (
        lax.ppermute(xe, axes, swap_pairs(sizes, "gx", 0)),
        lax.ppermute(xo, axes, swap_pairs(sizes, "gx", 1)),
        lax.ppermute(ye, axes, swap_pairs(sizes, "gy", 0)),
        lax.ppermute(yo, axes, swap_pairs(sizes, "gy", 1)),
    )


def swap_cores(x):
    count = lax.axis_size("blk")
    return lax.ppermute(x, "blk", [(i, count - 1 - i) for i in range(count)])


def face_kernel(p_ref, b_ref, xe_ref, xo_ref, ye_ref, yo_ref):
    cx, cy, _ = p_ref.shape
    for ref, takes_high in ((xe_ref, True), (xo_ref, False)):
        ref[:halo] = p_ref[pl.ds(start_of("gx", 0, cx - halo, takes_high), halo)]
        ref[halo:] = b_ref[pl.ds(start_of("gx", 0, cx - 2, takes_high), 2)]
    row = lax.broadcasted_iota(jnp.int32, (cx, tile, 1), 1)
    for ref, takes_high in ((ye_ref, True), (yo_ref, False)):
        start = pl.multiple_of(start_of("gy", 0, cy - tile, takes_high), tile)
        p, b = p_ref[:, pl.ds(start, tile), :], b_ref[:, pl.ds(start, tile), :]
        low = jnp.where(row < halo, p, pltpu.roll(b, halo, 1))
        high = jnp.where(row >= tile - halo, p, pltpu.roll(b, tile - halo, 1))
        ref[...] = jnp.where(start == 0, low, high)


def ahead(x, beyond, lane, step):
    lanes = x.shape[-1]
    if step > 0:
        return pltpu.roll(jnp.where(lane < step, beyond, x), lanes - step, x.ndim - 1)
    return pltpu.roll(jnp.where(lane >= lanes + step, beyond, x), -step, x.ndim - 1)


def depth_halo(x, lane):
    start = jnp.where(lax.axis_index("blk") == 0, 0, x.shape[-1] - halo)
    return jnp.where((lane >= start) & (lane < start + halo), x, 0.0)


def diff(a, b, c, d):
    return 27.0 * (a - b) - (c - d)


def fill(pad_ref, own_ref, low_x, high_x, low_y, high_y):
    cx, cy, _ = own_ref.shape
    wide = (pad_ref.shape[0] - cx) // 2
    pad_ref[:wide, tile : tile + cy] = low_x
    pad_ref[wide + cx :, tile : tile + cy] = high_x
    pad_ref[wide : wide + cx, :tile] = low_y
    pad_ref[wide : wide + cx, tile : tile + cy] = own_ref[...]
    pad_ref[wide : wide + cx, tile + cy :] = high_y


def operator(own_ref, other_ref, pad_ref, fx_ref, fy_ref, bx_ref, by_ref, bz_ref, bh_ref, finish):
    cx, cy, cz = own_ref.shape
    lane = lax.broadcasted_iota(jnp.int32, (cy, cz), 1)
    for f in range(cx + 3):
        v = [pad_ref[f + k, tile : tile + cy, :] for k in range(4)]
        fx_ref[f] = diff(v[2], v[1], v[3], v[0]) * bx_ref[f]
    long = cy + tile
    for i in range(cx):
        total = diff(fx_ref[i + 2], fx_ref[i + 1], fx_ref[i + 3], fx_ref[i])
        v = [pad_ref[i + halo, 5 + k : 5 + k + long, :] for k in range(4)]
        fy_ref[i % 2] = diff(v[2], v[1], v[3], v[0]) * by_ref[i]
        f = [fy_ref[i % 2, k : k + cy, :] for k in range(4)]
        total += diff(f[2], f[1], f[3], f[0])
        u = own_ref[i]
        h = depth_halo(other_ref[i], lane)
        fu = diff(ahead(u, h, lane, 1), u, ahead(u, h, lane, 2), ahead(u, h, lane, -1)) * bz_ref[i]
        fh = diff(ahead(h, u, lane, 1), h, ahead(h, u, lane, 2), ahead(h, u, lane, -1)) * bh_ref[i]
        total += diff(fu, ahead(fu, fh, lane, -1), ahead(fu, fh, lane, 1), ahead(fu, fh, lane, -2))
        finish(i, u, total)


def first_kernel(
    p_ref, b_ref, prev_ref, kappa_ref, xe_ref, xo_ref, ye_ref, yo_ref, po_ref, bo_ref,
    mid0_ref, bx_ref, by_ref, bz_ref, bh_ref, pad_ref, bpad_ref, fx_ref, fy_ref,
):
    cx, cy, cz = p_ref.shape
    low_x, high_x = low_and_high("gx", xe_ref[...], xo_ref[...])
    low_y, high_y = low_and_high("gy", ye_ref[...], yo_ref[...])
    fill(pad_ref, p_ref, low_x[:halo], high_x[:halo], low_y, high_y)
    fill(bpad_ref, b_ref, low_x[halo:], high_x[halo:], pltpu.roll(low_y, halo, 1), pltpu.roll(high_y, tile - halo, 1))
    lane = lax.broadcasted_iota(jnp.int32, (cy, cz), 1)
    for f in range(cx + 3):
        bx_ref[f] = bpad_ref[f, tile : tile + cy, :] + bpad_ref[f + 1, tile : tile + cy, :]
    long = cy + tile
    for i in range(cx):
        by_ref[i] = bpad_ref[i + 2, 6 : 6 + long, :] + bpad_ref[i + 2, 7 : 7 + long, :]
        u, h = b_ref[i], depth_halo(bo_ref[i], lane)
        bz_ref[i] = u + ahead(u, h, lane, 1)
        bh_ref[i] = h + ahead(h, u, lane, 1)

    def finish(i, u, total):
        mid0_ref[i] = 2.0 * u - prev_ref[i] + kappa_ref[i] * (lap_scale * total)

    operator(p_ref, po_ref, pad_ref, fx_ref, fy_ref, bx_ref, by_ref, bz_ref, bh_ref, finish)


def second_kernel(
    mid_ref, mid0_ref, p_ref, kappa_ref, xe_ref, xo_ref, ye_ref, yo_ref, mo_ref, bx_ref, by_ref, bz_ref, bh_ref, map_ref,
    next_ref, picked_ref, pad_ref, fx_ref, fy_ref,
):
    cx, cy, cz = p_ref.shape
    low_x, high_x = low_and_high("gx", xe_ref[...], xo_ref[...])
    low_y, high_y = low_and_high("gy", ye_ref[...], yo_ref[...])
    fill(pad_ref, mid_ref, low_x, high_x, low_y, high_y)

    def finish(i, u, total):
        next_ref[i] = 3.0 * u - mid0_ref[i] - p_ref[i] + kappa_ref[i] * (lap_scale * total)

    operator(mid_ref, mo_ref, pad_ref, fx_ref, fy_ref, bx_ref, by_ref, bz_ref, bh_ref, finish)
    picked_ref[...] = select_rows(map_ref[...], next_ref[...].reshape(cx * cy, cz)).reshape(picked_ref.shape)


def local(pressure, pressure_prev, buoyancy, kappa, hull_accel, row_block, row_column):
    groups = lax.axis_size("gx") * lax.axis_size("gy")
    rows, lanes = hull_accel.shape
    cap = 2 * rows // groups
    cx, cy, cz = pressure.shape
    slots, stride = groups * cap, cap + tile
    block = row_block.reshape(1, rows)
    column = row_column.reshape(1, rows)

    outgoing, place = run(
        functools.partial(pack_kernel, groups, cap),
        [shaped(groups * stride, lanes), shaped(1, rows)],
        block,
        column,
        hull_accel,
        flops=6 * groups * stride * rows * lanes,
    )
    got = lax.all_to_all(
        outgoing.reshape(groups, stride, lanes), ("gx", "gy"), split_axis=0, concat_axis=0, tiled=True
    )

    faces = run(
        face_kernel,
        [shaped(halo + 2, cy, cz)] * 2 + [shaped(cx, tile, cz)] * 2,
        pressure,
        buoyancy,
    )
    pads = [pltpu.VMEM((cx + 2 * halo, cy + 2 * tile, cz), f32)]
    fluxes = [pltpu.VMEM((cx + 3, cy, cz), f32), pltpu.VMEM((2, cy + tile, cz), f32)]
    mid0, *faced = run(
        first_kernel,
        [
            shaped(cx, cy, cz),
            shaped(cx + 3, cy, cz),
            shaped(cx, cy + tile, cz),
            shaped(cx, cy, cz),
            shaped(cx, cy, cz),
        ],
        pressure,
        buoyancy,
        pressure_prev,
        kappa,
        *exchange(*faces),
        swap_cores(pressure),
        swap_cores(buoyancy),
        flops=100 * cx * cy * cz,
        scratch=pads + [pltpu.VMEM((cx + 4, cy + 2 * tile, cz), f32)] + fluxes,
    )
    (unpack_map,) = run(
        functools.partial(unpack_map_kernel, lanes), [shaped(rows, slots, dtype=bf16)], place, flops=rows * slots
    )

    mid, *mid_faces = run(
        functools.partial(mid_kernel, cap),
        [shaped(cx, cy, cz)] + [shaped(halo, cy, cz)] * 2 + [shaped(cx, tile, cz)] * 2,
        got,
        mid0,
        kappa,
        flops=6 * cx * cy * slots * lanes,
        scratch=[pltpu.VMEM((cx * cy, slots), bf16)],
    )
    (gather_map,) = run(
        functools.partial(gather_map_kernel, cap, cx * cy),
        [shaped(slots, cx * cy, dtype=bf16)],
        got,
        flops=slots * cx * cy,
    )
    pressure_next, picked = run(
        second_kernel,
        [shaped(cx, cy, cz), shaped(groups, cap, lanes)],
        mid,
        mid0,
        pressure,
        kappa,
        *exchange(*mid_faces),
        swap_cores(mid),
        *faced,
        gather_map,
        flops=100 * cx * cy * cz + 6 * slots * cx * cy * lanes,
        scratch=pads + fluxes,
    )
    returned = lax.all_to_all(picked, ("gx", "gy"), split_axis=0, concat_axis=0, tiled=True)
    (hull_pressure,) = run(unpack_kernel, [shaped(rows, lanes)], unpack_map, returned, flops=6 * rows * slots * lanes)
    return pressure_next, hull_pressure


def solution(mesh):
    cells = P("gx", "gy", "blk")
    rows = P(("gx", "gy", "blk"), None)
    return jax.shard_map(
        local,
        mesh=mesh,
        in_specs=(cells, cells, cells, cells, rows, rows, rows),
        out_specs=(cells, rows),
        check_vma=False,
    )
```

```python
import functools
import math

import jax
import jax.numpy as jnp
from jax import lax
from jax.experimental import pallas as pl
from jax.experimental.pallas import tpu as pltpu
from jax.sharding import PartitionSpec as P

courant_sq = 0.05
source_gain = 0.5
lap_scale = courant_sq * 0.5 / (24.0 * 24.0)
halo = 3
tile = 8
f32 = jnp.float32
bf16 = jnp.bfloat16
VMEM_LIMIT = 16 << 20


def run(kernel, outs, *args, flops=0, scratch=(), in_space=pltpu.VMEM):
    size = sum(4 * math.prod(a.shape) for a in (*args, *outs))
    spec = pl.BlockSpec(memory_space=pltpu.VMEM)
    return pl.pallas_call(
        kernel,
        out_shape=outs,
        in_specs=[pl.BlockSpec(memory_space=in_space)] * len(args),
        out_specs=[spec] * len(outs),
        scratch_shapes=list(scratch),
        compiler_params=pltpu.CompilerParams(vmem_limit_bytes=VMEM_LIMIT),
        cost_estimate=pl.CostEstimate(flops=flops, bytes_accessed=size, transcendentals=0),
    )(*args)


def shaped(*shape, dtype=f32):
    return jax.ShapeDtypeStruct(shape, dtype)


def dot(a, b, contract=((1,), (0,))):
    return lax.dot_general(a, b, (contract, ((), ())), preferred_element_type=f32)


def parts_of(x):
    high = x.astype(bf16)
    rest = x - high.astype(f32)
    middle = rest.astype(bf16)
    low = (rest - middle.astype(f32)).astype(bf16)
    return jnp.concatenate([high, middle, low], axis=1)


def select_rows(one_hot, x):
    lanes = x.shape[1]
    y = dot(one_hot, parts_of(x))
    return y[:, :lanes] + y[:, lanes : 2 * lanes] + y[:, 2 * lanes :]


def one_hot_of(index, shape, dim):
    return jnp.where(lax.broadcasted_iota(jnp.int32, shape, dim) == index, 1.0, 0.0).astype(bf16)


def as_column(row):
    n = row.shape[1]
    diagonal = lax.broadcasted_iota(jnp.int32, (n, n), 0) == lax.broadcasted_iota(jnp.int32, (n, n), 1)
    return jnp.sum(jnp.where(diagonal, row, 0.0), axis=1, keepdims=True)


def pack_kernel(groups, cap, block_hbm, column_hbm, accel_hbm, out_ref, place_ref, block_ref, column_ref, accel_ref, sems):
    copies = [
        pltpu.make_async_copy(src, dst, sems.at[i])
        for i, (src, dst) in enumerate(
            ((block_hbm, block_ref), (column_hbm, column_ref), (accel_hbm, accel_ref))
        )
    ]
    for copy in copies:
        copy.start()
    rows, lanes = accel_ref.shape
    stride = cap + 1
    before = lax.broadcasted_iota(jnp.int32, (rows, rows), 0) < lax.broadcasted_iota(jnp.int32, (rows, rows), 1)
    before = jnp.where(before, 1.0, 0.0).astype(bf16)
    for copy in copies:
        copy.wait()
    block = block_ref[...]
    column = column_ref[...] + 1
    named = lax.broadcasted_iota(jnp.int32, (groups, rows), 0) == block
    matches = jnp.where(named, 1.0, 0.0).astype(bf16)
    earlier = dot(matches, before)
    slot = jnp.sum(jnp.where(named, earlier, 0.0), axis=0, keepdims=True).astype(jnp.int32)
    place_ref[...] = (block * cap + slot).astype(f32)
    out_ref[...] = select_rows(one_hot_of(block * stride + slot, (groups * stride, rows), 0), accel_ref[...])
    at_slot = lax.broadcasted_iota(jnp.int32, (lanes, rows), 0) % cap == slot
    high = jnp.where(at_slot, column // 32, 0).astype(f32).astype(bf16)
    low = jnp.where(at_slot, column % 32, 0).astype(f32).astype(bf16)
    columns = dot(matches, high, ((1,), (1,))) * 32.0 + dot(matches, low, ((1,), (1,)))
    for g in range(groups):
        out_ref[g * stride + cap : (g + 1) * stride, :] = columns[g : g + 1]


def column_rows(got_ref, cap):
    lanes = got_ref.shape[1]
    stride = cap + 1
    groups = got_ref.shape[0] // stride
    per = lanes // cap
    lane = lax.broadcasted_iota(jnp.int32, (1, lanes), 1) // cap
    rows = []
    for g in range(0, groups, per):
        row = got_ref[g * stride + cap : (g + 1) * stride, :]
        for k in range(1, per):
            row = jnp.where(lane == k, got_ref[(g + k) * stride + cap : (g + k + 1) * stride, :], row)
        rows.append(row - 1.0)
    return rows


def mid_kernel(cap, got_ref, mid0_ref, kappa_ref, mid_ref, xe_ref, xo_ref, ye_ref, yo_ref, spread_ref, rows_ref):
    lanes = got_ref.shape[1]
    groups = got_ref.shape[0] // (cap + 1)
    cx, cy, cz = mid0_ref.shape
    for at, row in enumerate(column_rows(got_ref, cap)):
        spread_ref[:, at * lanes : (at + 1) * lanes] = one_hot_of(row.astype(jnp.int32), (cx * cy, lanes), 0)
    for g in range(groups):
        rows_ref[g * cap : (g + 1) * cap, :] = got_ref[g * (cap + 1) : (g + 1) * (cap + 1) - 1, :]
    source = select_rows(spread_ref[...], rows_ref[...]).reshape(cx, cy, cz)
    mid_ref[...] = mid0_ref[...] + kappa_ref[...] * (source_gain * source)
    send_faces(((mid_ref, halo),), xe_ref, xo_ref, ye_ref, yo_ref)


def unpack_map_kernel(lanes, place_ref, map_ref):
    rows, slots = map_ref.shape
    for at in range(0, rows, lanes):
        column = as_column(place_ref[:, at : at + lanes]).astype(jnp.int32)
        map_ref[at : at + lanes, :] = one_hot_of(column, (lanes, slots), 1)


def unpack_kernel(map_ref, returned_ref, out_ref):
    slots = map_ref.shape[1]
    out_ref[...] = select_rows(map_ref[...], returned_ref[...].reshape(slots, -1))


def even_at(axis):
    return lax.axis_index(axis) % 2 == 0


def y_row(ref, j):
    cx, cy, cz = ref.shape
    return ref.reshape(cx * cy, cz)[pl.ds(j, cx, stride=cy), :]


def send_faces(fields, xe_ref, xo_ref, ye_ref, yo_ref):
    at = 0
    for ref, width in fields:
        cx, cy, _ = ref.shape
        even = even_at("gx")
        xe_ref[at : at + width] = ref[pl.ds(jnp.where(even, cx - width, 0), width)]
        xo_ref[at : at + width] = ref[pl.ds(jnp.where(even, 0, cx - width), width)]
        even = even_at("gy")
        for k in range(width):
            low, high = y_row(ref, k), y_row(ref, cy - width + k)
            ye_ref[at + k] = jnp.where(even, high, low)
            yo_ref[at + k] = jnp.where(even, low, high)
        at += width


def low_and_high(axis, from_even, from_odd):
    at = lax.axis_index(axis)
    even = at % 2 == 0
    low = jnp.where(at > 0, jnp.where(even, from_odd, from_even), 0.0)
    high = jnp.where(at < lax.axis_size(axis) - 1, jnp.where(even, from_even, from_odd), 0.0)
    return low, high


def swap_pairs(sizes, axis, first):
    num_gx, num_gy, num_blk = sizes
    pairs = []
    for x in range(num_gx):
        for y in range(num_gy):
            for b in range(num_blk):
                at, count = (x, num_gx) if axis == "gx" else (y, num_gy)
                other = at + 1 if at % 2 == first else at - 1
                if 0 <= other < count:
                    to = (other, y, b) if axis == "gx" else (x, other, b)
                else:
                    to = (x, y, num_blk - 1 - b)
                pairs.append(((x * num_gy + y) * num_blk + b, (to[0] * num_gy + to[1]) * num_blk + to[2]))
    return pairs


def exchange(xe, xo, ye, yo):
    axes = ("gx", "gy", "blk")
    sizes = tuple(lax.axis_size(a) for a in axes)
    yo = lax.ppermute(yo, axes, swap_pairs(sizes, "gy", 1))
    xo = lax.ppermute(xo, axes, swap_pairs(sizes, "gx", 1))
    xe = lax.ppermute(xe, axes, swap_pairs(sizes, "gx", 0))
    ye = lax.ppermute(ye, axes, swap_pairs(sizes, "gy", 0))
    return xe, xo, ye, yo


def swap_cores(x):
    count = lax.axis_size("blk")
    return lax.ppermute(x, "blk", [(i, count - 1 - i) for i in range(count)])


def face_kernel(p_ref, b_ref, xe_ref, xo_ref, ye_ref, yo_ref):
    send_faces(((p_ref, halo), (b_ref, 2)), xe_ref, xo_ref, ye_ref, yo_ref)


def ahead(x, beyond, lane, step):
    lanes = x.shape[-1]
    if step > 0:
        return pltpu.roll(jnp.where(lane < step, beyond, x), lanes - step, x.ndim - 1)
    return pltpu.roll(jnp.where(lane >= lanes + step, beyond, x), -step, x.ndim - 1)


def diff(a, b, c, d):
    near = (a if b is None else -b if a is None else a - b) * 27.0
    near = near if c is None else near - c
    return near if d is None else near + d


def inner(v_ref, b_ref, vo_ref, bo_ref, vpad_ref, bpad_ref, fx_ref, fy_ref, finish):
    cx, cy, cz = v_ref.shape
    lane = lax.broadcasted_iota(jnp.int32, (cy, cz), 1)
    last = lax.broadcasted_iota(jnp.int32, (cy, cz), 0) == cy - 1
    start = jnp.where(lax.axis_index("blk") == 0, 0, cz - halo)
    near = (lane >= start) & (lane < start + halo)
    for ref in (vpad_ref, bpad_ref, fy_ref):
        ref[:, :tile] = jnp.zeros((ref.shape[0], tile, cz), f32)
        ref[:, tile + cy :] = jnp.zeros((ref.shape[0], tile, cz), f32)
    vpad_ref[:, tile : tile + cy] = v_ref[...]
    bpad_ref[:, tile : tile + cy] = b_ref[...]

    def plane(ref, i, count):
        return ref[i] if 0 <= i < count else None

    for i in range(cx - 1):
        v = [plane(v_ref, i + k, cx) for k in (-1, 0, 1, 2)]
        fx_ref[i] = diff(v[2], v[1], v[3], v[0]) * (b_ref[i] + b_ref[i + 1])
    for i in range(cx):
        f = [plane(fx_ref, i + k, cx - 1) for k in (-2, -1, 0, 1)]
        total = diff(f[2], f[1], f[3], f[0])
        v = [vpad_ref[i, tile + k : tile + k + cy, :] for k in (-1, 0, 1, 2)]
        b = jnp.where(last, 0.0, b_ref[i] + bpad_ref[i, tile + 1 : tile + 1 + cy, :])
        fy = diff(v[2], v[1], v[3], v[0]) * b
        fy_ref[i % 2, tile : tile + cy, :] = fy
        f = [fy_ref[i % 2, tile + k : tile + k + cy, :] for k in (-2, -1, 1)]
        total += diff(fy, f[1], f[2], f[0])
        u, h = v_ref[i], jnp.where(near, vo_ref[i], 0.0)
        bu, bh = b_ref[i], jnp.where(near, bo_ref[i], 0.0)
        fu = diff(ahead(u, h, lane, 1), u, ahead(u, h, lane, 2), ahead(u, h, lane, -1)) * (bu + ahead(bu, bh, lane, 1))
        fh = diff(ahead(h, u, lane, 1), h, ahead(h, u, lane, 2), ahead(h, u, lane, -1)) * (bh + ahead(bh, bu, lane, 1))
        total += diff(fu, ahead(fu, fh, lane, -1), ahead(fu, fh, lane, 1), ahead(fu, fh, lane, -2))
        finish(i, u, total)


def edge(v0, v1, w1, w2, w3, b0, b1, b3):
    f3 = diff(w1, w2, v0, w3) * b3
    f1 = diff(v0, w1, v1, w2) * b1
    d0 = w1 * b0
    return 27.0 * (d0 - f1) + f3, f1 - 27.0 * d0, d0


def add_edges(out_ref, v_ref, b_ref, kappa_ref, low_x, high_x, low_y, high_y, bx, by):
    cx, cy, cz = v_ref.shape
    flat_out = out_ref.reshape(cx * cy, cz)
    sides = ((low_x, low_y, 0, 1, 0), (high_x, high_y, -1, -1, 2))
    for x, y, first, step, at in sides:
        w = (x[0], x[1], x[2])[:: -step]
        i = first % cx
        terms = edge(v_ref[i], v_ref[i + step], *w, b_ref[i] + b_ref[i + step], bx[at], bx[at + 1])
        for k, term in enumerate(terms):
            out_ref[i + k * step] += kappa_ref[i + k * step] * (lap_scale * term)
    for x, y, first, step, at in sides:
        w = (y[0], y[1], y[2])[:: -step]
        j = first % cy
        v0, v1, b = y_row(v_ref, j), y_row(v_ref, j + step), y_row(b_ref, j) + y_row(b_ref, j + step)
        terms = edge(v0, v1, *w, b, by[at], by[at + 1])
        for k, term in enumerate(terms):
            to = pl.ds(j + k * step, cx, stride=cy)
            flat_out[to, :] = flat_out[to, :] + y_row(kappa_ref, j + k * step) * (lap_scale * term)


def first_inner_kernel(p_ref, b_ref, prev_ref, kappa_ref, po_ref, bo_ref, out_ref, *scratch):
    def finish(i, u, total):
        out_ref[i] = 2.0 * u - prev_ref[i] + kappa_ref[i] * (lap_scale * total)

    inner(p_ref, b_ref, po_ref, bo_ref, *scratch, finish)


def first_edge_kernel(part_ref, p_ref, b_ref, kappa_ref, xe_ref, xo_ref, ye_ref, yo_ref, mid0_ref, bx_ref, by_ref):
    cx, cy, _ = p_ref.shape
    low_x, high_x = low_and_high("gx", xe_ref[...], xo_ref[...])
    low_y, high_y = low_and_high("gy", ye_ref[...], yo_ref[...])
    bx_ref[0] = low_x[4] + b_ref[0]
    bx_ref[1] = low_x[3] + low_x[4]
    bx_ref[2] = high_x[3] + b_ref[cx - 1]
    bx_ref[3] = high_x[3] + high_x[4]
    by_ref[0] = low_y[4] + y_row(b_ref, 0)
    by_ref[1] = low_y[3] + low_y[4]
    by_ref[2] = high_y[3] + y_row(b_ref, cy - 1)
    by_ref[3] = high_y[3] + high_y[4]
    mid0_ref[...] = part_ref[...]
    add_edges(mid0_ref, p_ref, b_ref, kappa_ref, low_x, high_x, low_y, high_y, bx_ref, by_ref)


def second_inner_kernel(
    cap, mid_ref, mid0_ref, p_ref, b_ref, kappa_ref, mo_ref, bo_ref, got_ref, out_ref, map_ref, *scratch
):
    cx, cy, _ = p_ref.shape
    lanes = got_ref.shape[1]

    def finish(i, u, total):
        out_ref[i] = 3.0 * u - mid0_ref[i] - p_ref[i] + kappa_ref[i] * (lap_scale * total)

    inner(mid_ref, b_ref, mo_ref, bo_ref, *scratch, finish)
    for at, row in enumerate(column_rows(got_ref, cap)):
        column = as_column(row).astype(jnp.int32)
        map_ref[at * lanes : (at + 1) * lanes, :] = one_hot_of(column, (lanes, cx * cy), 1)


def second_edge_kernel(
    part_ref, mid_ref, b_ref, kappa_ref, bx_ref, by_ref, map_ref, xe_ref, xo_ref, ye_ref, yo_ref, next_ref, picked_ref
):
    cx, cy, cz = mid_ref.shape
    low_x, high_x = low_and_high("gx", xe_ref[...], xo_ref[...])
    low_y, high_y = low_and_high("gy", ye_ref[...], yo_ref[...])
    next_ref[...] = part_ref[...]
    add_edges(next_ref, mid_ref, b_ref, kappa_ref, low_x, high_x, low_y, high_y, bx_ref, by_ref)
    picked_ref[...] = select_rows(map_ref[...], next_ref[...].reshape(cx * cy, cz)).reshape(picked_ref.shape)


def local(pressure, pressure_prev, buoyancy, kappa, hull_accel, row_block, row_column):
    groups = lax.axis_size("gx") * lax.axis_size("gy")
    rows, lanes = hull_accel.shape
    cap = 2 * rows // groups
    cx, cy, cz = pressure.shape
    slots, stride = groups * cap, cap + 1
    cells = shaped(cx, cy, cz)

    in_hbm = [pltpu.with_memory_space_constraint(a, pltpu.HBM) for a in (
        row_block.reshape(1, rows), row_column.reshape(1, rows), hull_accel)]
    outgoing, place = run(
        functools.partial(pack_kernel, groups, cap),
        [pltpu.VMEM((groups * stride, lanes), f32), shaped(1, rows)],
        *in_hbm,
        in_space=pl.ANY,
        flops=6 * groups * stride * rows * lanes,
        scratch=[pltpu.VMEM(a.shape, a.dtype) for a in in_hbm] + [pltpu.SemaphoreType.DMA((3,))],
    )
    got = lax.all_to_all(
        outgoing.reshape(groups, stride, 1, lanes), ("gx", "gy"), split_axis=0, concat_axis=0, tiled=True
    ).reshape(groups * stride, lanes)

    faces = run(
        face_kernel,
        [shaped(halo + 2, cy, cz)] * 2 + [shaped(halo + 2, cx, cz)] * 2,
        pressure,
        buoyancy,
    )
    beyond = exchange(*faces)
    other_b = swap_cores(buoyancy)
    scratch = [pltpu.VMEM((cx, cy + 2 * tile, cz), f32)] * 2 + [
        pltpu.VMEM((cx, cy, cz), f32),
        pltpu.VMEM((2, cy + 2 * tile, cz), f32),
    ]
    (part,) = run(
        first_inner_kernel,
        [cells],
        pressure,
        buoyancy,
        pressure_prev,
        kappa,
        swap_cores(pressure),
        other_b,
        flops=100 * cx * cy * cz,
        scratch=scratch,
    )
    mid0, bx, by = run(
        first_edge_kernel, [cells, shaped(4, cy, cz), shaped(4, cx, cz)], part, pressure, buoyancy, kappa, *beyond
    )

    mid, *mid_faces = run(
        functools.partial(mid_kernel, cap),
        [cells] + [shaped(halo, cy, cz)] * 2 + [shaped(halo, cx, cz)] * 2,
        got,
        mid0,
        kappa,
        flops=6 * cx * cy * slots * lanes,
        scratch=[pltpu.VMEM((cx * cy, slots), bf16), pltpu.VMEM((slots, lanes), f32)],
    )
    other_mid = swap_cores(mid)
    mid_beyond = exchange(*mid_faces)
    part, gather_map = run(
        functools.partial(second_inner_kernel, cap),
        [cells, shaped(slots, cx * cy, dtype=bf16)],
        mid,
        mid0,
        pressure,
        buoyancy,
        kappa,
        other_mid,
        other_b,
        got,
        flops=100 * cx * cy * cz,
        scratch=scratch,
    )
    pressure_next, picked = run(
        second_edge_kernel,
        [pltpu.VMEM((cx, cy, cz), f32), pltpu.VMEM((groups, cap, lanes), f32)],
        part,
        mid,
        buoyancy,
        kappa,
        bx,
        by,
        gather_map,
        *mid_beyond,
        flops=6 * slots * cx * cy * lanes,
    )
    returned = lax.all_to_all(picked, ("gx", "gy"), split_axis=0, concat_axis=0, tiled=True)
    (unpack_map,) = run(
        functools.partial(unpack_map_kernel, lanes), [shaped(rows, slots, dtype=bf16)], place, flops=rows * slots
    )
    (hull_pressure,) = run(unpack_kernel, [shaped(rows, lanes)], unpack_map, returned, flops=6 * rows * slots * lanes)
    return pressure_next, hull_pressure


def solution(mesh):
    cells = P("gx", "gy", "blk")
    rows = P(("gx", "gy", "blk"), None)
    return jax.shard_map(
        local,
        mesh=mesh,
        in_specs=(cells, cells, cells, cells, rows, rows, rows),
        out_specs=(cells, rows),
        check_vma=False,
    )
```

```python
import functools
import math

import jax
import jax.numpy as jnp
from jax import lax
from jax.experimental import pallas as pl
from jax.experimental.pallas import tpu as pltpu
from jax.sharding import PartitionSpec as P

courant_sq = 0.05
source_gain = 0.5
lap_scale = courant_sq * 0.5 / (24.0 * 24.0)
halo = 3
tile = 8
f32 = jnp.float32
bf16 = jnp.bfloat16
VMEM_LIMIT = 16 << 20
early = 10**11


def run(kernel, outs, *args, flops=0, scratch=(), in_space=pltpu.VMEM):
    size = sum(4 * math.prod(a.shape) for a in (*args, *outs))
    spec = pl.BlockSpec(memory_space=pltpu.VMEM)
    return pl.pallas_call(
        kernel,
        out_shape=outs,
        in_specs=[pl.BlockSpec(memory_space=in_space)] * len(args),
        out_specs=[spec] * len(outs),
        scratch_shapes=list(scratch),
        compiler_params=pltpu.CompilerParams(vmem_limit_bytes=VMEM_LIMIT),
        cost_estimate=pl.CostEstimate(flops=flops, bytes_accessed=size, transcendentals=0),
    )(*args)


def shaped(*shape, dtype=f32):
    return jax.ShapeDtypeStruct(shape, dtype)


def dot(a, b, contract=((1,), (0,))):
    return lax.dot_general(a, b, (contract, ((), ())), preferred_element_type=f32)


def parts_of(x):
    high = x.astype(bf16)
    return jnp.concatenate([high, (x - high.astype(f32)).astype(bf16)], axis=1)


def select_rows(one_hot, x):
    lanes = x.shape[1]
    y = dot(one_hot, parts_of(x))
    return y[:, :lanes] + y[:, lanes:]


def one_hot_of(index, shape, dim):
    return jnp.where(lax.broadcasted_iota(jnp.int32, shape, dim) == index, 1.0, 0.0).astype(bf16)


def as_column(row):
    n = row.shape[1]
    diagonal = lax.broadcasted_iota(jnp.int32, (n, n), 0) == lax.broadcasted_iota(jnp.int32, (n, n), 1)
    return jnp.sum(jnp.where(diagonal, row, 0.0), axis=1, keepdims=True)


def slot_kernel(
    groups, cap, block_hbm, column_hbm, accel_hbm, p_hbm, b_hbm,
    place_ref, columns_ref, accel_ref, xe_ref, xo_ref, block_ref, column_ref, sems,
):
    cx, even = p_hbm.shape[0], even_at("gx")
    moves = [(block_hbm, block_ref), (column_hbm, column_ref), (accel_hbm, accel_ref)]
    for field, width, at in ((p_hbm, halo, 0), (b_hbm, 2, halo)):
        moves.append((field.at[pl.ds(jnp.where(even, cx - width, 0), width)], xe_ref.at[pl.ds(at, width)]))
        moves.append((field.at[pl.ds(jnp.where(even, 0, cx - width), width)], xo_ref.at[pl.ds(at, width)]))
    copies = [pltpu.make_async_copy(src, dst, sems.at[i]) for i, (src, dst) in enumerate(moves)]
    for copy in copies:
        copy.start()
    rows, lanes = accel_ref.shape
    before = lax.broadcasted_iota(jnp.int32, (rows, rows), 0) < lax.broadcasted_iota(jnp.int32, (rows, rows), 1)
    before = jnp.where(before, 1.0, 0.0).astype(bf16)
    copies[0].wait()
    copies[1].wait()
    block = block_ref[...]
    column = column_ref[...] + 1
    named = lax.broadcasted_iota(jnp.int32, (groups, rows), 0) == block
    matches = jnp.where(named, 1.0, 0.0).astype(bf16)
    earlier = dot(matches, before)
    slot = jnp.sum(jnp.where(named, earlier, 0.0), axis=0, keepdims=True).astype(jnp.int32)
    place_ref[...] = block * (cap + 1) + slot
    at_slot = lax.broadcasted_iota(jnp.int32, (lanes, rows), 0) % cap == slot
    high = jnp.where(at_slot, column // 32, 0).astype(f32).astype(bf16)
    low = jnp.where(at_slot, column % 32, 0).astype(f32).astype(bf16)
    columns_ref[...] = dot(matches, high, ((1,), (1,))) * 32.0 + dot(matches, low, ((1,), (1,)))
    for copy in copies[2:]:
        copy.wait()


def pack_kernel(cap, place_ref, columns_ref, accel_ref, out_ref, slot_ref):
    rows = accel_ref.shape[0]
    groups = columns_ref.shape[0]
    stride = cap + 1
    place = place_ref[...]
    out_ref[...] = select_rows(one_hot_of(place, (groups * stride, rows), 0), accel_ref[...])
    for g in range(groups):
        out_ref[g * stride + cap : (g + 1) * stride, :] = columns_ref[g : g + 1, :]
    slot_ref[...] = (place - place // stride).astype(f32)


def column_rows(got_ref, cap):
    lanes = got_ref.shape[1]
    stride = cap + 1
    groups = got_ref.shape[0] // stride
    per = lanes // cap
    lane = lax.broadcasted_iota(jnp.int32, (1, lanes), 1) // cap
    rows = []
    for g in range(0, groups, per):
        row = got_ref[g * stride + cap : (g + 1) * stride, :]
        for k in range(1, per):
            row = jnp.where(lane == k, got_ref[(g + k) * stride + cap : (g + k + 1) * stride, :], row)
        rows.append(row - 1.0)
    return rows


def mid_kernel(cap, got_ref, mid0_ref, kappa_ref, mid_ref, xe_ref, xo_ref, ye_ref, yo_ref, spread_ref, rows_ref):
    lanes = got_ref.shape[1]
    groups = got_ref.shape[0] // (cap + 1)
    cx, cy, cz = mid0_ref.shape
    for at, row in enumerate(column_rows(got_ref, cap)):
        spread_ref[:, at * lanes : (at + 1) * lanes] = one_hot_of(row.astype(jnp.int32), (cx * cy, lanes), 0)
    for g in range(groups):
        rows_ref[g * cap : (g + 1) * cap, :] = got_ref[g * (cap + 1) : (g + 1) * (cap + 1) - 1, :]
    source = select_rows(spread_ref[...], rows_ref[...]).reshape(cx, cy, cz)
    mid_ref[...] = mid0_ref[...] + kappa_ref[...] * (source_gain * source)
    send_planes(mid_ref, halo, xe_ref, xo_ref)
    send_rows(((mid_ref, halo),), ye_ref, yo_ref)


def unpack_kernel(map_ref, returned_ref, out_ref):
    slots = map_ref.shape[1]
    out_ref[...] = select_rows(map_ref[...], returned_ref[...].reshape(slots, -1))


def even_at(axis):
    return lax.axis_index(axis) % 2 == 0


def y_row(ref, j):
    cx, cy, cz = ref.shape
    return ref.reshape(cx * cy, cz)[pl.ds(j, cx, stride=cy), :]


def send_planes(ref, width, xe_ref, xo_ref):
    cx, even = ref.shape[0], even_at("gx")
    xe_ref[...] = ref[pl.ds(jnp.where(even, cx - width, 0), width)]
    xo_ref[...] = ref[pl.ds(jnp.where(even, 0, cx - width), width)]


def send_rows(fields, ye_ref, yo_ref):
    at, even = 0, even_at("gy")
    for ref, width in fields:
        cy = ref.shape[1]
        for k in range(width):
            low, high = y_row(ref, k), y_row(ref, cy - width + k)
            ye_ref[at + k] = jnp.where(even, high, low)
            yo_ref[at + k] = jnp.where(even, low, high)
        at += width


def low_and_high(axis, from_even, from_odd):
    at = lax.axis_index(axis)
    even = at % 2 == 0
    low = jnp.where(at > 0, jnp.where(even, from_odd, from_even), 0.0)
    high = jnp.where(at < lax.axis_size(axis) - 1, jnp.where(even, from_even, from_odd), 0.0)
    return low, high


def swap_pairs(sizes, axis, first):
    num_gx, num_gy, num_blk = sizes
    pairs = []
    for x in range(num_gx):
        for y in range(num_gy):
            for b in range(num_blk):
                at, count = (x, num_gx) if axis == "gx" else (y, num_gy)
                other = at + 1 if at % 2 == first else at - 1
                if 0 <= other < count:
                    to = (other, y, b) if axis == "gx" else (x, other, b)
                else:
                    to = (x, y, num_blk - 1 - b)
                pairs.append(((x * num_gy + y) * num_blk + b, (to[0] * num_gy + to[1]) * num_blk + to[2]))
    return pairs


def exchange(axis, to_even, to_odd):
    axes = ("gx", "gy", "blk")
    sizes = tuple(lax.axis_size(a) for a in axes)
    to_odd = lax.ppermute(to_odd, axes, swap_pairs(sizes, axis, 1))
    return lax.ppermute(to_even, axes, swap_pairs(sizes, axis, 0)), to_odd


def swap_cores(x):
    count = lax.axis_size("blk")
    return lax.ppermute(x, "blk", [(i, count - 1 - i) for i in range(count)])


def row_face_kernel(p_ref, b_ref, slot_ref, xe_ref, xo_ref, ye_ref, yo_ref, p_out_ref, b_out_ref, bx_ref, map_ref):
    cx, _, lanes = p_ref.shape
    send_rows(((p_ref, halo), (b_ref, 2)), ye_ref, yo_ref)
    p_out_ref[...] = p_ref[...]
    b_out_ref[...] = b_ref[...]
    low, high = low_and_high("gx", xe_ref[halo:], xo_ref[halo:])
    bx_ref[0] = low[1] + b_ref[0]
    bx_ref[1] = low[0] + low[1]
    bx_ref[2] = high[0] + b_ref[cx - 1]
    bx_ref[3] = high[0] + high[1]
    rows, slots = map_ref.shape
    for at in range(0, rows, lanes):
        column = as_column(slot_ref[:, at : at + lanes]).astype(jnp.int32)
        map_ref[at : at + lanes, :] = one_hot_of(column, (lanes, slots), 1)


def ahead(x, beyond, lane, step):
    lanes = x.shape[-1]
    if step > 0:
        return pltpu.roll(jnp.where(lane < step, beyond, x), lanes - step, x.ndim - 1)
    return pltpu.roll(jnp.where(lane >= lanes + step, beyond, x), -step, x.ndim - 1)


def diff(a, b, c, d):
    near = (a if b is None else -b if a is None else a - b) * 27.0
    near = near if c is None else near - c
    return near if d is None else near + d


def inner(v_ref, b_ref, vo_ref, bo_ref, vpad_ref, bpad_ref, fx_ref, fy_ref, finish):
    cx, cy, cz = v_ref.shape
    lane = lax.broadcasted_iota(jnp.int32, (cy, cz), 1)
    last = lax.broadcasted_iota(jnp.int32, (cy, cz), 0) == cy - 1
    start = jnp.where(lax.axis_index("blk") == 0, 0, cz - halo)
    near = (lane >= start) & (lane < start + halo)
    for ref in (vpad_ref, bpad_ref, fy_ref):
        ref[:, :tile] = jnp.zeros((ref.shape[0], tile, cz), f32)
        ref[:, tile + cy :] = jnp.zeros((ref.shape[0], tile, cz), f32)
    vpad_ref[:, tile : tile + cy] = v_ref[...]
    bpad_ref[:, tile : tile + cy] = b_ref[...]

    def plane(ref, i, count):
        return ref[i] if 0 <= i < count else None

    for i in range(cx - 1):
        v = [plane(v_ref, i + k, cx) for k in (-1, 0, 1, 2)]
        fx_ref[i] = diff(v[2], v[1], v[3], v[0]) * (b_ref[i] + b_ref[i + 1])
    for i in range(cx):
        f = [plane(fx_ref, i + k, cx - 1) for k in (-2, -1, 0, 1)]
        total = diff(f[2], f[1], f[3], f[0])
        v = [vpad_ref[i, tile + k : tile + k + cy, :] for k in (-1, 0, 1, 2)]
        b = jnp.where(last, 0.0, b_ref[i] + bpad_ref[i, tile + 1 : tile + 1 + cy, :])
        fy = diff(v[2], v[1], v[3], v[0]) * b
        fy_ref[i % 2, tile : tile + cy, :] = fy
        f = [fy_ref[i % 2, tile + k : tile + k + cy, :] for k in (-2, -1, 1)]
        total += diff(fy, f[1], f[2], f[0])
        u, h = v_ref[i], jnp.where(near, vo_ref[i], 0.0)
        bu, bh = b_ref[i], jnp.where(near, bo_ref[i], 0.0)
        fu = diff(ahead(u, h, lane, 1), u, ahead(u, h, lane, 2), ahead(u, h, lane, -1)) * (bu + ahead(bu, bh, lane, 1))
        fh = diff(ahead(h, u, lane, 1), h, ahead(h, u, lane, 2), ahead(h, u, lane, -1)) * (bh + ahead(bh, bu, lane, 1))
        total += diff(fu, ahead(fu, fh, lane, -1), ahead(fu, fh, lane, 1), ahead(fu, fh, lane, -2))
        finish(i, u, total)


def edge(v0, v1, w1, w2, w3, b0, b1, b3):
    f3 = diff(w1, w2, v0, w3) * b3
    f1 = diff(v0, w1, v1, w2) * b1
    d0 = w1 * b0
    return 27.0 * (d0 - f1) + f3, f1 - 27.0 * d0, d0


def add_edges(out_ref, v_ref, b_ref, kappa_ref, low_x, high_x, low_y, high_y, bx, by):
    cx, cy, cz = v_ref.shape
    flat_out = out_ref.reshape(cx * cy, cz)
    sides = ((low_x, low_y, 0, 1, 0), (high_x, high_y, -1, -1, 2))
    for x, y, first, step, at in sides:
        w = (x[0], x[1], x[2])[:: -step]
        i = first % cx
        terms = edge(v_ref[i], v_ref[i + step], *w, b_ref[i] + b_ref[i + step], bx[at], bx[at + 1])
        for k, term in enumerate(terms):
            out_ref[i + k * step] += kappa_ref[i + k * step] * (lap_scale * term)
    for x, y, first, step, at in sides:
        w = (y[0], y[1], y[2])[:: -step]
        j = first % cy
        v0, v1, b = y_row(v_ref, j), y_row(v_ref, j + step), y_row(b_ref, j) + y_row(b_ref, j + step)
        terms = edge(v0, v1, *w, b, by[at], by[at + 1])
        for k, term in enumerate(terms):
            to = pl.ds(j + k * step, cx, stride=cy)
            flat_out[to, :] = flat_out[to, :] + y_row(kappa_ref, j + k * step) * (lap_scale * term)


def first_inner_kernel(p_ref, b_ref, prev_ref, kappa_ref, po_ref, bo_ref, out_ref, *scratch):
    def finish(i, u, total):
        out_ref[i] = 2.0 * u - prev_ref[i] + kappa_ref[i] * (lap_scale * total)

    inner(p_ref, b_ref, po_ref, bo_ref, *scratch, finish)


def first_edge_kernel(part_ref, p_ref, b_ref, kappa_ref, bx_ref, xe_ref, xo_ref, ye_ref, yo_ref, mid0_ref, by_ref):
    cy = p_ref.shape[1]
    low_x, high_x = low_and_high("gx", xe_ref[:halo], xo_ref[:halo])
    low_y, high_y = low_and_high("gy", ye_ref[...], yo_ref[...])
    by_ref[0] = low_y[4] + y_row(b_ref, 0)
    by_ref[1] = low_y[3] + low_y[4]
    by_ref[2] = high_y[3] + y_row(b_ref, cy - 1)
    by_ref[3] = high_y[3] + high_y[4]
    mid0_ref[...] = part_ref[...]
    add_edges(mid0_ref, p_ref, b_ref, kappa_ref, low_x, high_x, low_y, high_y, bx_ref, by_ref)


def second_inner_kernel(
    cap, mid_ref, mid0_ref, p_ref, b_ref, kappa_ref, mo_ref, bo_ref, got_ref, out_ref, map_ref, *scratch
):
    cx, cy, _ = p_ref.shape
    lanes = got_ref.shape[1]

    def finish(i, u, total):
        out_ref[i] = 3.0 * u - mid0_ref[i] - p_ref[i] + kappa_ref[i] * (lap_scale * total)

    inner(mid_ref, b_ref, mo_ref, bo_ref, *scratch, finish)
    for at, row in enumerate(column_rows(got_ref, cap)):
        column = as_column(row).astype(jnp.int32)
        map_ref[at * lanes : (at + 1) * lanes, :] = one_hot_of(column, (lanes, cx * cy), 1)


def second_edge_kernel(
    part_ref, mid_ref, b_ref, kappa_ref, bx_ref, by_ref, map_ref, xe_ref, xo_ref, ye_ref, yo_ref, next_ref, picked_ref
):
    cx, cy, cz = mid_ref.shape
    low_x, high_x = low_and_high("gx", xe_ref[...], xo_ref[...])
    low_y, high_y = low_and_high("gy", ye_ref[...], yo_ref[...])
    next_ref[...] = part_ref[...]
    add_edges(next_ref, mid_ref, b_ref, kappa_ref, low_x, high_x, low_y, high_y, bx_ref, by_ref)
    picked_ref[...] = select_rows(map_ref[...], next_ref[...].reshape(cx * cy, cz)).reshape(picked_ref.shape)


def local(pressure, pressure_prev, buoyancy, kappa, hull_accel, row_block, row_column):
    groups = lax.axis_size("gx") * lax.axis_size("gy")
    rows, lanes = hull_accel.shape
    cap = 2 * rows // groups
    cx, cy, cz = pressure.shape
    slots, stride = groups * cap, cap + 1
    cells = shaped(cx, cy, cz)

    in_hbm = [pltpu.with_memory_space_constraint(a, pltpu.HBM) for a in (
        row_block.reshape(1, rows), row_column.reshape(1, rows), hull_accel, pressure, buoyancy)]
    place, columns, accel, xe, xo = run(
        functools.partial(slot_kernel, groups, cap),
        [shaped(1, rows, dtype=jnp.int32), shaped(groups, lanes)] + [pltpu.VMEM(o, f32) for o in ((rows, lanes),) + ((halo + 2, cy, cz),) * 2],
        *in_hbm,
        in_space=pl.ANY,
        flops=2 * groups * rows * rows,
        scratch=[pltpu.VMEM((1, rows), jnp.int32)] * 2 + [pltpu.SemaphoreType.DMA((7,))],
    )
    outgoing, slot = run(
        functools.partial(pack_kernel, cap),
        [shaped(groups * stride, lanes), shaped(1, rows)],
        place,
        columns,
        accel,
        flops=4 * groups * stride * rows * lanes,
    )
    got = lax.all_to_all(
        outgoing.reshape(groups, stride, 1, lanes), ("gx", "gy"), split_axis=0, concat_axis=0, tiled=True
    ).reshape(groups * stride, lanes)

    xe, xo = exchange("gx", xe, xo)
    ye, yo, p_out, b_out, bx, unpack_map = run(
        row_face_kernel,
        [shaped(halo + 2, cx, cz)] * 2 + [cells] * 2 + [shaped(4, cy, cz), shaped(rows, slots, dtype=bf16)],
        pressure,
        buoyancy,
        slot,
        xe,
        xo,
        flops=early,
    )
    other_b = swap_cores(b_out)
    ye, yo = exchange("gy", ye, yo)
    scratch = [pltpu.VMEM((cx, cy + 2 * tile, cz), f32)] * 2 + [
        pltpu.VMEM((cx, cy, cz), f32),
        pltpu.VMEM((2, cy + 2 * tile, cz), f32),
    ]
    (part,) = run(
        first_inner_kernel,
        [cells],
        pressure,
        buoyancy,
        pressure_prev,
        kappa,
        swap_cores(p_out),
        other_b,
        flops=100 * cx * cy * cz,
        scratch=scratch,
    )
    mid0, by = run(
        first_edge_kernel, [cells, shaped(4, cx, cz)], part, pressure, buoyancy, kappa, bx, xe, xo, ye, yo
    )

    mid, *mid_faces = run(
        functools.partial(mid_kernel, cap),
        [cells] + [shaped(halo, cy, cz)] * 2 + [shaped(halo, cx, cz)] * 2,
        got,
        mid0,
        kappa,
        flops=6 * cx * cy * slots * lanes,
        scratch=[pltpu.VMEM((cx * cy, slots), bf16), pltpu.VMEM((slots, lanes), f32)],
    )
    other_mid = swap_cores(mid)
    mid_beyond = exchange("gx", *mid_faces[:2]) + exchange("gy", *mid_faces[2:])
    part, gather_map = run(
        functools.partial(second_inner_kernel, cap),
        [cells, shaped(slots, cx * cy, dtype=bf16)],
        mid,
        mid0,
        pressure,
        buoyancy,
        kappa,
        other_mid,
        other_b,
        got,
        flops=100 * cx * cy * cz,
        scratch=scratch,
    )
    pressure_next, picked = run(
        second_edge_kernel,
        [pltpu.VMEM((cx, cy, cz), f32), pltpu.VMEM((groups, cap, lanes), f32)],
        part,
        mid,
        buoyancy,
        kappa,
        bx,
        by,
        gather_map,
        *mid_beyond,
        flops=6 * slots * cx * cy * lanes,
    )
    returned = lax.all_to_all(picked, ("gx", "gy"), split_axis=0, concat_axis=0, tiled=True)
    (hull_pressure,) = run(unpack_kernel, [shaped(rows, lanes)], unpack_map, returned, flops=6 * rows * slots * lanes)
    return pressure_next, hull_pressure


def solution(mesh):
    cells = P("gx", "gy", "blk")
    rows = P(("gx", "gy", "blk"), None)
    return jax.shard_map(
        local,
        mesh=mesh,
        in_specs=(cells, cells, cells, cells, rows, rows, rows),
        out_specs=(cells, rows),
        check_vma=False,
    )
```

```python
import functools
import math

import jax
import jax.numpy as jnp
import numpy as np
from jax import lax
from jax.experimental import pallas as pl
from jax.experimental.pallas import tpu as pltpu
from jax.sharding import PartitionSpec as P

courant_sq = 0.05
source_gain = 0.5
lap_scale = courant_sq * 0.5 / (24.0 * 24.0)
halo = 3
tile = 8
f32 = jnp.float32
bf16 = jnp.bfloat16
VMEM_LIMIT = 16 << 20
early = 10**11
order_seeds = (205, 205)


def run(kernel, outs, *args, flops=0, scratch=(), in_space=pltpu.VMEM, out_space=pltpu.VMEM):
    size = sum(4 * math.prod(a.shape) for a in (*args, *outs))
    return pl.pallas_call(
        kernel,
        out_shape=outs,
        in_specs=[pl.BlockSpec(memory_space=in_space)] * len(args),
        out_specs=[
            pl.BlockSpec(memory_space=m) for m in (out_space if isinstance(out_space, list) else [out_space] * len(outs))
        ],
        scratch_shapes=list(scratch),
        compiler_params=pltpu.CompilerParams(vmem_limit_bytes=VMEM_LIMIT),
        cost_estimate=pl.CostEstimate(flops=flops, bytes_accessed=size, transcendentals=0),
    )(*args)


def shaped(*shape, dtype=f32):
    return jax.ShapeDtypeStruct(shape, dtype)


def dot(a, b, contract=((1,), (0,))):
    return lax.dot_general(a, b, (contract, ((), ())), preferred_element_type=f32)


def parts_of(x):
    high = x.astype(bf16)
    return jnp.concatenate([high, (x - high.astype(f32)).astype(bf16)], axis=1)


def select_rows(one_hot, x):
    lanes = x.shape[1]
    y = dot(one_hot, parts_of(x))
    return y[:, :lanes] + y[:, lanes:]


def one_hot_of(index, shape, dim):
    return jnp.where(lax.broadcasted_iota(jnp.int32, shape, dim) == index, 1.0, 0.0).astype(bf16)


def as_column(row):
    n = row.shape[1]
    diagonal = lax.broadcasted_iota(jnp.int32, (n, n), 0) == lax.broadcasted_iota(jnp.int32, (n, n), 1)
    return jnp.sum(jnp.where(diagonal, row, 0.0), axis=1, keepdims=True)


def send_orders(groups):
    return [[int(g) for g in np.random.default_rng(seed).permutation(groups)] for seed in order_seeds]


def exchange_rows(x, orders):
    num_blk = lax.axis_size("blk")
    members = [[g * num_blk + b for g in orders[b]] for b in range(num_blk)]
    return lax.all_to_all(
        x, ("gx", "gy", "blk"), split_axis=0, concat_axis=0, tiled=True, axis_index_groups=members
    )


def slot_kernel(
    orders, cap, block_hbm, column_hbm, accel_hbm, p_hbm, b_hbm,
    place_ref, columns_ref, accel_ref, xe_ref, xo_ref, block_ref, column_ref, sems,
):
    cx, even = p_hbm.shape[0], even_at("gx")
    moves = [(block_hbm, block_ref), (column_hbm, column_ref), (accel_hbm, accel_ref)]
    for field, width, at in ((p_hbm, halo, 0), (b_hbm, 2, halo)):
        moves.append((field.at[pl.ds(jnp.where(even, cx - width, 0), width)], xe_ref.at[pl.ds(at, width)]))
        moves.append((field.at[pl.ds(jnp.where(even, 0, cx - width), width)], xo_ref.at[pl.ds(at, width)]))
    copies = [pltpu.make_async_copy(src, dst, sems.at[i]) for i, (src, dst) in enumerate(moves)]
    for copy in copies:
        copy.start()
    rows, lanes = accel_ref.shape
    before = lax.broadcasted_iota(jnp.int32, (rows, rows), 0) < lax.broadcasted_iota(jnp.int32, (rows, rows), 1)
    before = jnp.where(before, 1.0, 0.0).astype(bf16)
    copies[0].wait()
    copies[1].wait()
    block = block_ref[...]
    column = column_ref[...] + 1
    groups = len(orders[0])
    rank = lax.broadcasted_iota(jnp.int32, (groups, rows), 0)
    first = lax.axis_index("blk") == 0
    holds = jnp.zeros((groups, 1), jnp.int32)
    for at, (one, other) in enumerate(zip(*orders)):
        holds = jnp.where(rank[:, :1] == at, jnp.where(first, one, other), holds)
    named = holds == block
    matches = jnp.where(named, 1.0, 0.0).astype(bf16)
    earlier = dot(matches, before)
    slot = jnp.sum(jnp.where(named, earlier, 0.0), axis=0, keepdims=True).astype(jnp.int32)
    place_ref[...] = jnp.sum(jnp.where(named, rank, 0), axis=0, keepdims=True) * (cap + 1) + slot
    at_slot = lax.broadcasted_iota(jnp.int32, (lanes, rows), 0) % cap == slot
    high = jnp.where(at_slot, column // 32, 0).astype(f32).astype(bf16)
    low = jnp.where(at_slot, column % 32, 0).astype(f32).astype(bf16)
    columns_ref[...] = dot(matches, high, ((1,), (1,))) * 32.0 + dot(matches, low, ((1,), (1,)))
    for copy in copies[2:]:
        copy.wait()


def pack_kernel(cap, place_ref, columns_ref, accel_ref, out_hbm, slot_ref, out_ref, sems):
    rows, lanes = accel_ref.shape
    stride = cap + 1
    total = out_ref.shape[0]
    chunks = sems.shape[0]
    chunk = total // chunks
    place = place_ref[...]
    parts = parts_of(accel_ref[...])
    copies = []
    for k in range(chunks):
        part = pl.ds(k * chunk, chunk)
        y = dot(one_hot_of(place - k * chunk, (chunk, rows), 0), parts)
        out_ref[part, :] = y[:, :lanes] + y[:, lanes:]
        for at in range(k * chunk, (k + 1) * chunk):
            if at % stride == cap:
                out_ref[at : at + 1, :] = columns_ref[at // stride : at // stride + 1, :]
        copies.append(pltpu.make_async_copy(out_ref.at[part], out_hbm.at[part], sems.at[k]))
        copies[k].start()
    slot_ref[...] = (place - place // stride).astype(f32)
    for copy in copies:
        copy.wait()


def column_rows(got_ref, cap):
    lanes = got_ref.shape[1]
    stride = cap + 1
    groups = got_ref.shape[0] // stride
    per = lanes // cap
    lane = lax.broadcasted_iota(jnp.int32, (1, lanes), 1) // cap
    rows = []
    for g in range(0, groups, per):
        row = got_ref[g * stride + cap : (g + 1) * stride, :]
        for k in range(1, per):
            row = jnp.where(lane == k, got_ref[(g + k) * stride + cap : (g + k + 1) * stride, :], row)
        rows.append(row - 1.0)
    return rows


def mid_kernel(cap, got_ref, mid0_ref, kappa_ref, mid_ref, xe_ref, xo_ref, ye_ref, yo_ref, spread_ref, rows_ref):
    lanes = got_ref.shape[1]
    groups = got_ref.shape[0] // (cap + 1)
    cx, cy, cz = mid0_ref.shape
    for at, row in enumerate(column_rows(got_ref, cap)):
        spread_ref[:, at * lanes : (at + 1) * lanes] = one_hot_of(row.astype(jnp.int32), (cx * cy, lanes), 0)
    for g in range(groups):
        rows_ref[g * cap : (g + 1) * cap, :] = got_ref[g * (cap + 1) : (g + 1) * (cap + 1) - 1, :]
    source = select_rows(spread_ref[...], rows_ref[...]).reshape(cx, cy, cz)
    mid_ref[...] = mid0_ref[...] + kappa_ref[...] * (source_gain * source)
    send_planes(mid_ref, halo, xe_ref, xo_ref)
    send_rows(((mid_ref, halo),), ye_ref, yo_ref)


def unpack_kernel(map_ref, returned_ref, next_ref, out_hbm, next_hbm, out_ref, sems):
    copies = [pltpu.make_async_copy(next_ref, next_hbm, sems.at[0])]
    copies[0].start()
    rows, slots = map_ref.shape
    lanes = out_ref.shape[1]
    parts = parts_of(returned_ref[...].reshape(slots, lanes))
    half = rows // 2
    for at in (0, half):
        part = pl.ds(at, half)
        y = dot(map_ref[part, :], parts)
        out_ref[part, :] = y[:, :lanes] + y[:, lanes:]
        copies.append(pltpu.make_async_copy(out_ref.at[part], out_hbm.at[part], sems.at[len(copies)]))
        copies[-1].start()
    for copy in copies:
        copy.wait()


def even_at(axis):
    return lax.axis_index(axis) % 2 == 0


def y_row(ref, j):
    cx, cy, cz = ref.shape
    return ref.reshape(cx * cy, cz)[pl.ds(j, cx, stride=cy), :]


def send_planes(ref, width, xe_ref, xo_ref):
    cx, even = ref.shape[0], even_at("gx")
    xe_ref[...] = ref[pl.ds(jnp.where(even, cx - width, 0), width)]
    xo_ref[...] = ref[pl.ds(jnp.where(even, 0, cx - width), width)]


def send_rows(fields, ye_ref, yo_ref):
    at, even = 0, even_at("gy")
    for ref, width in fields:
        cy = ref.shape[1]
        for k in range(width):
            low, high = y_row(ref, k), y_row(ref, cy - width + k)
            ye_ref[at + k] = jnp.where(even, high, low)
            yo_ref[at + k] = jnp.where(even, low, high)
        at += width


def low_and_high(axis, from_even, from_odd):
    at = lax.axis_index(axis)
    even = at % 2 == 0
    low = jnp.where(at > 0, jnp.where(even, from_odd, from_even), 0.0)
    high = jnp.where(at < lax.axis_size(axis) - 1, jnp.where(even, from_even, from_odd), 0.0)
    return low, high


def swap_pairs(sizes, axis, first):
    num_gx, num_gy, num_blk = sizes
    pairs = []
    for x in range(num_gx):
        for y in range(num_gy):
            for b in range(num_blk):
                at, count = (x, num_gx) if axis == "gx" else (y, num_gy)
                other = at + 1 if at % 2 == first else at - 1
                if 0 <= other < count:
                    to = (other, y, b) if axis == "gx" else (x, other, b)
                else:
                    to = (x, y, num_blk - 1 - b)
                pairs.append(((x * num_gy + y) * num_blk + b, (to[0] * num_gy + to[1]) * num_blk + to[2]))
    return pairs


def exchange(axis, to_even, to_odd):
    axes = ("gx", "gy", "blk")
    sizes = tuple(lax.axis_size(a) for a in axes)
    to_odd = lax.ppermute(to_odd, axes, swap_pairs(sizes, axis, 1))
    return lax.ppermute(to_even, axes, swap_pairs(sizes, axis, 0)), to_odd


def swap_cores(x):
    count = lax.axis_size("blk")
    return lax.ppermute(x, "blk", [(i, count - 1 - i) for i in range(count)])


def row_face_kernel(p_ref, b_ref, slot_ref, xe_ref, xo_ref, ye_ref, yo_ref, p_out_ref, b_out_ref, bx_ref, map_ref):
    cx, _, lanes = p_ref.shape
    send_rows(((p_ref, halo), (b_ref, 2)), ye_ref, yo_ref)
    p_out_ref[...] = p_ref[...]
    b_out_ref[...] = b_ref[...]
    low, high = low_and_high("gx", xe_ref[halo:], xo_ref[halo:])
    bx_ref[0] = low[1] + b_ref[0]
    bx_ref[1] = low[0] + low[1]
    bx_ref[2] = high[0] + b_ref[cx - 1]
    bx_ref[3] = high[0] + high[1]
    rows, slots = map_ref.shape
    for at in range(0, rows, lanes):
        column = as_column(slot_ref[:, at : at + lanes]).astype(jnp.int32)
        map_ref[at : at + lanes, :] = one_hot_of(column, (lanes, slots), 1)


def ahead(x, beyond, lane, step):
    lanes = x.shape[-1]
    if step > 0:
        return pltpu.roll(jnp.where(lane < step, beyond, x), lanes - step, x.ndim - 1)
    return pltpu.roll(jnp.where(lane >= lanes + step, beyond, x), -step, x.ndim - 1)


def diff(a, b, c, d):
    near = (a if b is None else -b if a is None else a - b) * 27.0
    near = near if c is None else near - c
    return near if d is None else near + d


def inner(v_ref, b_ref, vo_ref, bo_ref, vpad_ref, bpad_ref, fx_ref, fy_ref, finish):
    cx, cy, cz = v_ref.shape
    lane = lax.broadcasted_iota(jnp.int32, (cy, cz), 1)
    last = lax.broadcasted_iota(jnp.int32, (cy, cz), 0) == cy - 1
    start = jnp.where(lax.axis_index("blk") == 0, 0, cz - halo)
    near = (lane >= start) & (lane < start + halo)
    for ref in (vpad_ref, bpad_ref, fy_ref):
        ref[:, :tile] = jnp.zeros((ref.shape[0], tile, cz), f32)
        ref[:, tile + cy :] = jnp.zeros((ref.shape[0], tile, cz), f32)
    vpad_ref[:, tile : tile + cy] = v_ref[...]
    bpad_ref[:, tile : tile + cy] = b_ref[...]

    def plane(ref, i, count):
        return ref[i] if 0 <= i < count else None

    for i in range(cx - 1):
        v = [plane(v_ref, i + k, cx) for k in (-1, 0, 1, 2)]
        fx_ref[i] = diff(v[2], v[1], v[3], v[0]) * (b_ref[i] + b_ref[i + 1])
    for i in range(cx):
        f = [plane(fx_ref, i + k, cx - 1) for k in (-2, -1, 0, 1)]
        total = diff(f[2], f[1], f[3], f[0])
        v = [vpad_ref[i, tile + k : tile + k + cy, :] for k in (-1, 0, 1, 2)]
        b = jnp.where(last, 0.0, b_ref[i] + bpad_ref[i, tile + 1 : tile + 1 + cy, :])
        fy = diff(v[2], v[1], v[3], v[0]) * b
        fy_ref[i % 2, tile : tile + cy, :] = fy
        f = [fy_ref[i % 2, tile + k : tile + k + cy, :] for k in (-2, -1, 1)]
        total += diff(fy, f[1], f[2], f[0])
        u, h = v_ref[i], jnp.where(near, vo_ref[i], 0.0)
        bu, bh = b_ref[i], jnp.where(near, bo_ref[i], 0.0)
        fu = diff(ahead(u, h, lane, 1), u, ahead(u, h, lane, 2), ahead(u, h, lane, -1)) * (bu + ahead(bu, bh, lane, 1))
        fh = diff(ahead(h, u, lane, 1), h, ahead(h, u, lane, 2), ahead(h, u, lane, -1)) * (bh + ahead(bh, bu, lane, 1))
        total += diff(fu, ahead(fu, fh, lane, -1), ahead(fu, fh, lane, 1), ahead(fu, fh, lane, -2))
        finish(i, u, total)


def edge(v0, v1, w1, w2, w3, b0, b1, b3):
    f3 = diff(w1, w2, v0, w3) * b3
    f1 = diff(v0, w1, v1, w2) * b1
    d0 = w1 * b0
    return 27.0 * (d0 - f1) + f3, f1 - 27.0 * d0, d0


def add_edges(out_ref, v_ref, b_ref, kappa_ref, low_x, high_x, low_y, high_y, bx, by):
    cx, cy, cz = v_ref.shape
    flat_out = out_ref.reshape(cx * cy, cz)
    sides = ((low_x, low_y, 0, 1, 0), (high_x, high_y, -1, -1, 2))
    for x, y, first, step, at in sides:
        w = (x[0], x[1], x[2])[:: -step]
        i = first % cx
        terms = edge(v_ref[i], v_ref[i + step], *w, b_ref[i] + b_ref[i + step], bx[at], bx[at + 1])
        for k, term in enumerate(terms):
            out_ref[i + k * step] += kappa_ref[i + k * step] * (lap_scale * term)
    for x, y, first, step, at in sides:
        w = (y[0], y[1], y[2])[:: -step]
        j = first % cy
        v0, v1, b = y_row(v_ref, j), y_row(v_ref, j + step), y_row(b_ref, j) + y_row(b_ref, j + step)
        terms = edge(v0, v1, *w, b, by[at], by[at + 1])
        for k, term in enumerate(terms):
            to = pl.ds(j + k * step, cx, stride=cy)
            flat_out[to, :] = flat_out[to, :] + y_row(kappa_ref, j + k * step) * (lap_scale * term)


def first_inner_kernel(p_ref, b_ref, prev_ref, kappa_ref, po_ref, bo_ref, out_ref, *scratch):
    def finish(i, u, total):
        out_ref[i] = 2.0 * u - prev_ref[i] + kappa_ref[i] * (lap_scale * total)

    inner(p_ref, b_ref, po_ref, bo_ref, *scratch, finish)


def first_edge_kernel(part_ref, p_ref, b_ref, kappa_ref, bx_ref, xe_ref, xo_ref, ye_ref, yo_ref, mid0_ref, by_ref):
    cy = p_ref.shape[1]
    low_x, high_x = low_and_high("gx", xe_ref[:halo], xo_ref[:halo])
    low_y, high_y = low_and_high("gy", ye_ref[...], yo_ref[...])
    by_ref[0] = low_y[4] + y_row(b_ref, 0)
    by_ref[1] = low_y[3] + low_y[4]
    by_ref[2] = high_y[3] + y_row(b_ref, cy - 1)
    by_ref[3] = high_y[3] + high_y[4]
    mid0_ref[...] = part_ref[...]
    add_edges(mid0_ref, p_ref, b_ref, kappa_ref, low_x, high_x, low_y, high_y, bx_ref, by_ref)


def second_inner_kernel(
    cap, mid_ref, mid0_ref, p_ref, b_ref, kappa_ref, mo_ref, bo_ref, got_ref, out_ref, map_ref, *scratch
):
    cx, cy, _ = p_ref.shape
    lanes = got_ref.shape[1]

    def finish(i, u, total):
        out_ref[i] = 3.0 * u - mid0_ref[i] - p_ref[i] + kappa_ref[i] * (lap_scale * total)

    inner(mid_ref, b_ref, mo_ref, bo_ref, *scratch, finish)
    for at, row in enumerate(column_rows(got_ref, cap)):
        column = as_column(row).astype(jnp.int32)
        map_ref[at * lanes : (at + 1) * lanes, :] = one_hot_of(column, (lanes, cx * cy), 1)


def second_edge_kernel(
    part_ref, mid_ref, b_ref, kappa_ref, bx_ref, by_ref, map_ref, xe_ref, xo_ref, ye_ref, yo_ref, next_ref, picked_ref
):
    cx, cy, cz = mid_ref.shape
    low_x, high_x = low_and_high("gx", xe_ref[...], xo_ref[...])
    low_y, high_y = low_and_high("gy", ye_ref[...], yo_ref[...])
    next_ref[...] = part_ref[...]
    add_edges(next_ref, mid_ref, b_ref, kappa_ref, low_x, high_x, low_y, high_y, bx_ref, by_ref)
    picked_ref[...] = select_rows(map_ref[...], next_ref[...].reshape(cx * cy, cz)).reshape(picked_ref.shape)


def local(pressure, pressure_prev, buoyancy, kappa, hull_accel, row_block, row_column):
    groups = lax.axis_size("gx") * lax.axis_size("gy")
    orders = send_orders(groups)
    rows, lanes = hull_accel.shape
    cap = 2 * rows // groups
    cx, cy, cz = pressure.shape
    slots, stride = groups * cap, cap + 1
    cells = shaped(cx, cy, cz)

    in_hbm = [pltpu.with_memory_space_constraint(a, pltpu.HBM) for a in (
        row_block.reshape(1, rows), row_column.reshape(1, rows), hull_accel, pressure, buoyancy)]
    place, columns, accel, xe, xo = run(
        functools.partial(slot_kernel, orders, cap),
        [shaped(1, rows, dtype=jnp.int32), shaped(groups, lanes)] + [pltpu.VMEM(o, f32) for o in ((rows, lanes),) + ((halo + 2, cy, cz),) * 2],
        *in_hbm,
        in_space=pl.ANY,
        flops=2 * groups * rows * rows,
        scratch=[pltpu.VMEM((1, rows), jnp.int32)] * 2 + [pltpu.SemaphoreType.DMA((7,))],
    )
    chunks = max(n for n in range(1, 6) if groups * stride % (n * tile) == 0)
    outgoing, slot = run(
        functools.partial(pack_kernel, cap),
        [shaped(groups * stride, lanes), shaped(1, rows)],
        place,
        columns,
        accel,
        out_space=[pl.ANY, pltpu.VMEM],
        flops=4 * groups * stride * rows * lanes,
        scratch=[pltpu.VMEM((groups * stride, lanes), f32), pltpu.SemaphoreType.DMA((chunks,))],
    )
    got = exchange_rows(outgoing.reshape(groups, stride, 1, lanes), orders).reshape(groups * stride, lanes)

    xe, xo = exchange("gx", xe, xo)
    ye, yo, p_out, b_out, bx, unpack_map = run(
        row_face_kernel,
        [shaped(halo + 2, cx, cz)] * 2 + [cells] * 2 + [shaped(4, cy, cz), shaped(rows, slots, dtype=bf16)],
        pressure,
        buoyancy,
        slot,
        xe,
        xo,
        flops=early,
    )
    other_b = swap_cores(b_out)
    ye, yo = exchange("gy", ye, yo)
    scratch = [pltpu.VMEM((cx, cy + 2 * tile, cz), f32)] * 2 + [
        pltpu.VMEM((cx, cy, cz), f32),
        pltpu.VMEM((2, cy + 2 * tile, cz), f32),
    ]
    (part,) = run(
        first_inner_kernel,
        [cells],
        pressure,
        buoyancy,
        pressure_prev,
        kappa,
        swap_cores(p_out),
        other_b,
        flops=100 * cx * cy * cz,
        scratch=scratch,
    )
    mid0, by = run(
        first_edge_kernel, [cells, shaped(4, cx, cz)], part, pressure, buoyancy, kappa, bx, xe, xo, ye, yo
    )

    mid, *mid_faces = run(
        functools.partial(mid_kernel, cap),
        [cells] + [shaped(halo, cy, cz)] * 2 + [shaped(halo, cx, cz)] * 2,
        got,
        mid0,
        kappa,
        flops=6 * cx * cy * slots * lanes,
        scratch=[pltpu.VMEM((cx * cy, slots), bf16), pltpu.VMEM((slots, lanes), f32)],
    )
    other_mid = swap_cores(mid)
    mid_beyond = exchange("gx", *mid_faces[:2]) + exchange("gy", *mid_faces[2:])
    part, gather_map = run(
        functools.partial(second_inner_kernel, cap),
        [cells, shaped(slots, cx * cy, dtype=bf16)],
        mid,
        mid0,
        pressure,
        buoyancy,
        kappa,
        other_mid,
        other_b,
        got,
        flops=100 * cx * cy * cz,
        scratch=scratch,
    )
    pressure_next, picked = run(
        second_edge_kernel,
        [pltpu.VMEM((cx, cy, cz), f32), pltpu.VMEM((groups, cap, lanes), f32)],
        part,
        mid,
        buoyancy,
        kappa,
        bx,
        by,
        gather_map,
        *mid_beyond,
        flops=6 * slots * cx * cy * lanes,
    )
    returned = exchange_rows(picked, orders)
    hull_pressure, pressure_next = run(
        unpack_kernel,
        [shaped(rows, lanes), cells],
        unpack_map,
        returned,
        pressure_next,
        out_space=pl.ANY,
        flops=4 * rows * slots * lanes,
        scratch=[pltpu.VMEM((rows, lanes), f32), pltpu.SemaphoreType.DMA((3,))],
    )
    return pressure_next, hull_pressure


def solution(mesh):
    cells = P("gx", "gy", "blk")
    rows = P(("gx", "gy", "blk"), None)
    return jax.shard_map(
        local,
        mesh=mesh,
        in_specs=(cells, cells, cells, cells, rows, rows, rows),
        out_specs=(cells, rows),
        check_vma=False,
    )
```

```python
import functools
import math

import jax
import jax.numpy as jnp
import numpy as np
from jax import lax
from jax.experimental import pallas as pl
from jax.experimental.pallas import tpu as pltpu
from jax.sharding import PartitionSpec as P

courant_sq = 0.05
source_gain = 0.5
lap_scale = courant_sq * 0.5 / (24.0 * 24.0)
halo = 3
tile = 8
f32 = jnp.float32
bf16 = jnp.bfloat16
VMEM_LIMIT = 16 << 20
early = 10**11
order_seeds = (56, 205)


def run(kernel, outs, *args, flops=0, scratch=(), in_space=pltpu.VMEM, out_space=pltpu.VMEM):
    size = sum(4 * math.prod(a.shape) for a in (*args, *outs))
    return pl.pallas_call(
        kernel,
        out_shape=outs,
        in_specs=[pl.BlockSpec(memory_space=in_space)] * len(args),
        out_specs=[
            pl.BlockSpec(memory_space=m) for m in (out_space if isinstance(out_space, list) else [out_space] * len(outs))
        ],
        scratch_shapes=list(scratch),
        compiler_params=pltpu.CompilerParams(vmem_limit_bytes=VMEM_LIMIT),
        cost_estimate=pl.CostEstimate(flops=flops, bytes_accessed=size, transcendentals=0),
    )(*args)


def shaped(*shape, dtype=f32):
    return jax.ShapeDtypeStruct(shape, dtype)


def dot(a, b, contract=((1,), (0,))):
    return lax.dot_general(a, b, (contract, ((), ())), preferred_element_type=f32)


def parts_of(x):
    high = x.astype(bf16)
    return jnp.concatenate([high, (x - high.astype(f32)).astype(bf16)], axis=1)


def select_rows(one_hot, x):
    lanes = x.shape[1]
    y = dot(one_hot, parts_of(x))
    return y[:, :lanes] + y[:, lanes:]


def one_hot_of(index, shape, dim):
    short = jnp.int16
    places = lax.broadcasted_iota(jnp.int32, shape, dim).astype(short)
    return jnp.where(places == index.astype(short), bf16(1), bf16(0))


def as_column(row):
    n = row.shape[1]
    diagonal = lax.broadcasted_iota(jnp.int32, (n, n), 0) == lax.broadcasted_iota(jnp.int32, (n, n), 1)
    return jnp.sum(jnp.where(diagonal, row, 0.0), axis=1, keepdims=True)


def send_orders(groups):
    return [[int(g) for g in np.random.default_rng(seed).permutation(groups)] for seed in order_seeds]


def exchange_rows(x, orders):
    num_blk = lax.axis_size("blk")
    members = [[g * num_blk + b for g in orders[b]] for b in range(num_blk)]
    return lax.all_to_all(
        x, ("gx", "gy", "blk"), split_axis=0, concat_axis=0, tiled=True, axis_index_groups=members
    )


def slot_kernel(
    orders, cap, block_hbm, column_hbm, accel_hbm, p_hbm, b_hbm,
    place_ref, columns_ref, accel_ref, xe_ref, xo_ref, block_ref, column_ref, sems,
):
    cx, even = p_hbm.shape[0], even_at("gx")
    moves = [(block_hbm, block_ref), (column_hbm, column_ref), (accel_hbm, accel_ref)]
    for field, width, at in ((p_hbm, halo, 0), (b_hbm, 2, halo)):
        moves.append((field.at[pl.ds(jnp.where(even, cx - width, 0), width)], xe_ref.at[pl.ds(at, width)]))
        moves.append((field.at[pl.ds(jnp.where(even, 0, cx - width), width)], xo_ref.at[pl.ds(at, width)]))
    copies = [pltpu.make_async_copy(src, dst, sems.at[i]) for i, (src, dst) in enumerate(moves)]
    for copy in copies:
        copy.start()
    rows, lanes = accel_ref.shape
    before = lax.broadcasted_iota(jnp.int32, (rows, rows), 0) < lax.broadcasted_iota(jnp.int32, (rows, rows), 1)
    before = jnp.where(before, 1.0, 0.0).astype(bf16)
    copies[0].wait()
    copies[1].wait()
    block = block_ref[...]
    column = column_ref[...] + 1
    groups = len(orders[0])
    rank = lax.broadcasted_iota(jnp.int32, (groups, rows), 0)
    first = lax.axis_index("blk") == 0
    holds = jnp.zeros((groups, 1), jnp.int32)
    for at, (one, other) in enumerate(zip(*orders)):
        holds = jnp.where(rank[:, :1] == at, jnp.where(first, one, other), holds)
    named = holds == block
    matches = jnp.where(named, 1.0, 0.0).astype(bf16)
    earlier = dot(matches, before)
    slot = jnp.sum(jnp.where(named, earlier, 0.0), axis=0, keepdims=True).astype(jnp.int32)
    place_ref[...] = jnp.sum(jnp.where(named, rank, 0), axis=0, keepdims=True) * (cap + 1) + slot
    at_slot = lax.broadcasted_iota(jnp.int32, (lanes, rows), 0) % cap == slot
    high = jnp.where(at_slot, column // 32, 0).astype(f32).astype(bf16)
    low = jnp.where(at_slot, column % 32, 0).astype(f32).astype(bf16)
    columns_ref[...] = dot(matches, high, ((1,), (1,))) * 32.0 + dot(matches, low, ((1,), (1,)))
    for copy in copies[2:]:
        copy.wait()


def pack_kernel(cap, place_ref, columns_ref, accel_ref, out_hbm, slot_ref, out_ref, sems):
    rows, lanes = accel_ref.shape
    stride = cap + 1
    total = out_ref.shape[0]
    chunks = sems.shape[0]
    chunk = total // chunks
    place = place_ref[...]
    parts = parts_of(accel_ref[...])
    copies = []
    for k in range(chunks):
        part = pl.ds(k * chunk, chunk)
        y = dot(one_hot_of(place - k * chunk, (chunk, rows), 0), parts)
        out_ref[part, :] = y[:, :lanes] + y[:, lanes:]
        for at in range(k * chunk, (k + 1) * chunk):
            if at % stride == cap:
                out_ref[at : at + 1, :] = columns_ref[at // stride : at // stride + 1, :]
        copies.append(pltpu.make_async_copy(out_ref.at[part], out_hbm.at[part], sems.at[k]))
        copies[k].start()
    slot_ref[...] = (place - place // stride).astype(f32)
    for copy in copies:
        copy.wait()


def column_rows(got_ref, cap):
    lanes = got_ref.shape[1]
    stride = cap + 1
    groups = got_ref.shape[0] // stride
    per = lanes // cap
    lane = lax.broadcasted_iota(jnp.int32, (1, lanes), 1) // cap
    rows = []
    for g in range(0, groups, per):
        row = got_ref[g * stride + cap : (g + 1) * stride, :]
        for k in range(1, per):
            row = jnp.where(lane == k, got_ref[(g + k) * stride + cap : (g + k + 1) * stride, :], row)
        rows.append(row - 1.0)
    return rows


def mid_kernel(cap, got_ref, mid0_ref, kappa_ref, mid_ref, xe_ref, xo_ref, ye_ref, yo_ref, spread_ref, rows_ref):
    lanes = got_ref.shape[1]
    groups = got_ref.shape[0] // (cap + 1)
    cx, cy, cz = mid0_ref.shape
    for at, row in enumerate(column_rows(got_ref, cap)):
        spread_ref[:, at * lanes : (at + 1) * lanes] = one_hot_of(row.astype(jnp.int32), (cx * cy, lanes), 0)
    for g in range(groups):
        rows_ref[g * cap : (g + 1) * cap, :] = got_ref[g * (cap + 1) : (g + 1) * (cap + 1) - 1, :]
    source = select_rows(spread_ref[...], rows_ref[...]).reshape(cx, cy, cz)
    mid_ref[...] = mid0_ref[...] + kappa_ref[...] * (source_gain * source)
    send_planes(mid_ref, halo, xe_ref, xo_ref)
    send_rows(((mid_ref, halo),), ye_ref, yo_ref)


def unpack_kernel(map_ref, returned_ref, next_ref, out_hbm, next_hbm, out_ref, sems):
    copies = [pltpu.make_async_copy(next_ref, next_hbm, sems.at[0])]
    copies[0].start()
    rows, slots = map_ref.shape
    lanes = out_ref.shape[1]
    parts = parts_of(returned_ref[...].reshape(slots, lanes))
    half = rows // 2
    for at in (0, half):
        part = pl.ds(at, half)
        y = dot(map_ref[part, :], parts)
        out_ref[part, :] = y[:, :lanes] + y[:, lanes:]
        copies.append(pltpu.make_async_copy(out_ref.at[part], out_hbm.at[part], sems.at[len(copies)]))
        copies[-1].start()
    for copy in copies:
        copy.wait()


def even_at(axis):
    return lax.axis_index(axis) % 2 == 0


def y_row(ref, j):
    cx, cy, cz = ref.shape
    return ref.reshape(cx * cy, cz)[pl.ds(j, cx, stride=cy), :]


def send_planes(ref, width, xe_ref, xo_ref):
    cx, even = ref.shape[0], even_at("gx")
    xe_ref[...] = ref[pl.ds(jnp.where(even, cx - width, 0), width)]
    xo_ref[...] = ref[pl.ds(jnp.where(even, 0, cx - width), width)]


def send_rows(fields, ye_ref, yo_ref):
    at, even = 0, even_at("gy")
    for ref, width in fields:
        cy = ref.shape[1]
        for k in range(width):
            low, high = y_row(ref, k), y_row(ref, cy - width + k)
            ye_ref[at + k] = jnp.where(even, high, low)
            yo_ref[at + k] = jnp.where(even, low, high)
        at += width


def low_and_high(axis, from_even, from_odd):
    at = lax.axis_index(axis)
    even = at % 2 == 0
    low = jnp.where(at > 0, jnp.where(even, from_odd, from_even), 0.0)
    high = jnp.where(at < lax.axis_size(axis) - 1, jnp.where(even, from_even, from_odd), 0.0)
    return low, high


def swap_pairs(sizes, axis, first):
    num_gx, num_gy, num_blk = sizes
    pairs = []
    for x in range(num_gx):
        for y in range(num_gy):
            for b in range(num_blk):
                at, count = (x, num_gx) if axis == "gx" else (y, num_gy)
                other = at + 1 if at % 2 == first else at - 1
                if 0 <= other < count:
                    to = (other, y, b) if axis == "gx" else (x, other, b)
                else:
                    to = (x, y, num_blk - 1 - b)
                pairs.append(((x * num_gy + y) * num_blk + b, (to[0] * num_gy + to[1]) * num_blk + to[2]))
    return pairs


def exchange(axis, to_even, to_odd):
    axes = ("gx", "gy", "blk")
    sizes = tuple(lax.axis_size(a) for a in axes)
    to_odd = lax.ppermute(to_odd, axes, swap_pairs(sizes, axis, 1))
    return lax.ppermute(to_even, axes, swap_pairs(sizes, axis, 0)), to_odd


def swap_cores(x):
    count = lax.axis_size("blk")
    return lax.ppermute(x, "blk", [(i, count - 1 - i) for i in range(count)])


def row_face_kernel(p_ref, b_ref, slot_ref, xe_ref, xo_ref, ye_ref, yo_ref, p_out_ref, b_out_ref, bx_ref, map_ref):
    cx, _, lanes = p_ref.shape
    send_rows(((p_ref, halo), (b_ref, 2)), ye_ref, yo_ref)
    p_out_ref[...] = p_ref[...]
    b_out_ref[...] = b_ref[...]
    low, high = low_and_high("gx", xe_ref[halo:], xo_ref[halo:])
    bx_ref[0] = low[1] + b_ref[0]
    bx_ref[1] = low[0] + low[1]
    bx_ref[2] = high[0] + b_ref[cx - 1]
    bx_ref[3] = high[0] + high[1]
    rows, slots = map_ref.shape
    for at in range(0, rows, lanes):
        column = as_column(slot_ref[:, at : at + lanes]).astype(jnp.int32)
        map_ref[at : at + lanes, :] = one_hot_of(column, (lanes, slots), 1)


def ahead(x, beyond, lane, step):
    lanes = x.shape[-1]
    if step > 0:
        return pltpu.roll(jnp.where(lane < step, beyond, x), lanes - step, x.ndim - 1)
    return pltpu.roll(jnp.where(lane >= lanes + step, beyond, x), -step, x.ndim - 1)


def diff(a, b, c, d):
    near = (a if b is None else -b if a is None else a - b) * 27.0
    near = near if c is None else near - c
    return near if d is None else near + d


def inner(v_ref, b_ref, vo_ref, bo_ref, vpad_ref, bpad_ref, fx_ref, fy_ref, finish):
    cx, cy, cz = v_ref.shape
    lane = lax.broadcasted_iota(jnp.int32, (cy, cz), 1)
    last = lax.broadcasted_iota(jnp.int32, (cy, cz), 0) == cy - 1
    start = jnp.where(lax.axis_index("blk") == 0, 0, cz - halo)
    near = (lane >= start) & (lane < start + halo)
    for ref in (vpad_ref, bpad_ref, fy_ref):
        ref[:, :tile] = jnp.zeros((ref.shape[0], tile, cz), f32)
        ref[:, tile + cy :] = jnp.zeros((ref.shape[0], tile, cz), f32)
    vpad_ref[:, tile : tile + cy] = v_ref[...]
    bpad_ref[:, tile : tile + cy] = b_ref[...]

    def plane(ref, i, count):
        return ref[i] if 0 <= i < count else None

    for i in range(cx - 1):
        v = [plane(v_ref, i + k, cx) for k in (-1, 0, 1, 2)]
        fx_ref[i] = diff(v[2], v[1], v[3], v[0]) * (b_ref[i] + b_ref[i + 1])
    for i in range(cx):
        f = [plane(fx_ref, i + k, cx - 1) for k in (-2, -1, 0, 1)]
        total = diff(f[2], f[1], f[3], f[0])
        v = [vpad_ref[i, tile + k : tile + k + cy, :] for k in (-1, 0, 1, 2)]
        b = jnp.where(last, 0.0, b_ref[i] + bpad_ref[i, tile + 1 : tile + 1 + cy, :])
        fy = diff(v[2], v[1], v[3], v[0]) * b
        fy_ref[i % 2, tile : tile + cy, :] = fy
        f = [fy_ref[i % 2, tile + k : tile + k + cy, :] for k in (-2, -1, 1)]
        total += diff(fy, f[1], f[2], f[0])
        u, h = v_ref[i], jnp.where(near, vo_ref[i], 0.0)
        bu, bh = b_ref[i], jnp.where(near, bo_ref[i], 0.0)
        fu = diff(ahead(u, h, lane, 1), u, ahead(u, h, lane, 2), ahead(u, h, lane, -1)) * (bu + ahead(bu, bh, lane, 1))
        fh = diff(ahead(h, u, lane, 1), h, ahead(h, u, lane, 2), ahead(h, u, lane, -1)) * (bh + ahead(bh, bu, lane, 1))
        total += diff(fu, ahead(fu, fh, lane, -1), ahead(fu, fh, lane, 1), ahead(fu, fh, lane, -2))
        finish(i, u, total)


def edge(v0, v1, w1, w2, w3, b0, b1, b3):
    f3 = diff(w1, w2, v0, w3) * b3
    f1 = diff(v0, w1, v1, w2) * b1
    d0 = w1 * b0
    return 27.0 * (d0 - f1) + f3, f1 - 27.0 * d0, d0


def add_edges(out_ref, v_ref, b_ref, kappa_ref, low_x, high_x, low_y, high_y, bx, by):
    cx, cy, cz = v_ref.shape
    flat_out = out_ref.reshape(cx * cy, cz)
    sides = ((low_x, low_y, 0, 1, 0), (high_x, high_y, -1, -1, 2))
    for x, y, first, step, at in sides:
        w = (x[0], x[1], x[2])[:: -step]
        i = first % cx
        terms = edge(v_ref[i], v_ref[i + step], *w, b_ref[i] + b_ref[i + step], bx[at], bx[at + 1])
        for k, term in enumerate(terms):
            out_ref[i + k * step] += kappa_ref[i + k * step] * (lap_scale * term)
    for x, y, first, step, at in sides:
        w = (y[0], y[1], y[2])[:: -step]
        j = first % cy
        v0, v1, b = y_row(v_ref, j), y_row(v_ref, j + step), y_row(b_ref, j) + y_row(b_ref, j + step)
        terms = edge(v0, v1, *w, b, by[at], by[at + 1])
        for k, term in enumerate(terms):
            to = pl.ds(j + k * step, cx, stride=cy)
            flat_out[to, :] = flat_out[to, :] + y_row(kappa_ref, j + k * step) * (lap_scale * term)


def first_inner_kernel(p_ref, b_ref, prev_ref, kappa_ref, po_ref, bo_ref, out_ref, *scratch):
    def finish(i, u, total):
        out_ref[i] = 2.0 * u - prev_ref[i] + kappa_ref[i] * (lap_scale * total)

    inner(p_ref, b_ref, po_ref, bo_ref, *scratch, finish)


def first_edge_kernel(part_ref, p_ref, b_ref, kappa_ref, bx_ref, xe_ref, xo_ref, ye_ref, yo_ref, mid0_ref, by_ref):
    cy = p_ref.shape[1]
    low_x, high_x = low_and_high("gx", xe_ref[:halo], xo_ref[:halo])
    low_y, high_y = low_and_high("gy", ye_ref[...], yo_ref[...])
    by_ref[0] = low_y[4] + y_row(b_ref, 0)
    by_ref[1] = low_y[3] + low_y[4]
    by_ref[2] = high_y[3] + y_row(b_ref, cy - 1)
    by_ref[3] = high_y[3] + high_y[4]
    mid0_ref[...] = part_ref[...]
    add_edges(mid0_ref, p_ref, b_ref, kappa_ref, low_x, high_x, low_y, high_y, bx_ref, by_ref)


def second_inner_kernel(
    cap, mid_ref, mid0_ref, p_ref, b_ref, kappa_ref, mo_ref, bo_ref, got_ref, out_ref, map_ref, *scratch
):
    cx, cy, _ = p_ref.shape
    lanes = got_ref.shape[1]

    def finish(i, u, total):
        out_ref[i] = 3.0 * u - mid0_ref[i] - p_ref[i] + kappa_ref[i] * (lap_scale * total)

    inner(mid_ref, b_ref, mo_ref, bo_ref, *scratch, finish)
    for at, row in enumerate(column_rows(got_ref, cap)):
        column = as_column(row).astype(jnp.int32)
        map_ref[at * lanes : (at + 1) * lanes, :] = one_hot_of(column, (lanes, cx * cy), 1)


def second_edge_kernel(
    part_ref, mid_ref, b_ref, kappa_ref, bx_ref, by_ref, map_ref, xe_ref, xo_ref, ye_ref, yo_ref, next_ref, picked_ref
):
    cx, cy, cz = mid_ref.shape
    low_x, high_x = low_and_high("gx", xe_ref[...], xo_ref[...])
    low_y, high_y = low_and_high("gy", ye_ref[...], yo_ref[...])
    next_ref[...] = part_ref[...]
    add_edges(next_ref, mid_ref, b_ref, kappa_ref, low_x, high_x, low_y, high_y, bx_ref, by_ref)
    picked_ref[...] = select_rows(map_ref[...], next_ref[...].reshape(cx * cy, cz)).reshape(picked_ref.shape)


def local(pressure, pressure_prev, buoyancy, kappa, hull_accel, row_block, row_column):
    groups = lax.axis_size("gx") * lax.axis_size("gy")
    orders = send_orders(groups)
    rows, lanes = hull_accel.shape
    cap = 2 * rows // groups
    cx, cy, cz = pressure.shape
    slots, stride = groups * cap, cap + 1
    cells = shaped(cx, cy, cz)

    in_hbm = [pltpu.with_memory_space_constraint(a, pltpu.HBM) for a in (
        row_block.reshape(1, rows), row_column.reshape(1, rows), hull_accel, pressure, buoyancy)]
    place, columns, accel, xe, xo = run(
        functools.partial(slot_kernel, orders, cap),
        [shaped(1, rows, dtype=jnp.int32), shaped(groups, lanes)] + [pltpu.VMEM(o, f32) for o in ((rows, lanes),) + ((halo + 2, cy, cz),) * 2],
        *in_hbm,
        in_space=pl.ANY,
        flops=2 * groups * rows * rows,
        scratch=[pltpu.VMEM((1, rows), jnp.int32)] * 2 + [pltpu.SemaphoreType.DMA((7,))],
    )
    chunks = max(n for n in range(1, 6) if groups * stride % (n * tile) == 0)
    outgoing, slot = run(
        functools.partial(pack_kernel, cap),
        [shaped(groups * stride, lanes), shaped(1, rows)],
        place,
        columns,
        accel,
        out_space=[pl.ANY, pltpu.VMEM],
        flops=4 * groups * stride * rows * lanes,
        scratch=[pltpu.VMEM((groups * stride, lanes), f32), pltpu.SemaphoreType.DMA((chunks,))],
    )
    got = exchange_rows(outgoing.reshape(groups, stride, 1, lanes), orders).reshape(groups * stride, lanes)

    xe, xo = exchange("gx", xe, xo)
    ye, yo, p_out, b_out, bx, unpack_map = run(
        row_face_kernel,
        [shaped(halo + 2, cx, cz)] * 2 + [cells] * 2 + [shaped(4, cy, cz), shaped(rows, slots, dtype=bf16)],
        pressure,
        buoyancy,
        slot,
        xe,
        xo,
        flops=early,
    )
    other_b = swap_cores(b_out)
    ye, yo = exchange("gy", ye, yo)
    scratch = [pltpu.VMEM((cx, cy + 2 * tile, cz), f32)] * 2 + [
        pltpu.VMEM((cx, cy, cz), f32),
        pltpu.VMEM((2, cy + 2 * tile, cz), f32),
    ]
    (part,) = run(
        first_inner_kernel,
        [cells],
        pressure,
        buoyancy,
        pressure_prev,
        kappa,
        swap_cores(p_out),
        other_b,
        flops=100 * cx * cy * cz,
        scratch=scratch,
    )
    mid0, by = run(
        first_edge_kernel, [cells, shaped(4, cx, cz)], part, pressure, buoyancy, kappa, bx, xe, xo, ye, yo
    )

    mid, *mid_faces = run(
        functools.partial(mid_kernel, cap),
        [cells] + [shaped(halo, cy, cz)] * 2 + [shaped(halo, cx, cz)] * 2,
        got,
        mid0,
        kappa,
        flops=6 * cx * cy * slots * lanes,
        scratch=[pltpu.VMEM((cx * cy, slots), bf16), pltpu.VMEM((slots, lanes), f32)],
    )
    other_mid = swap_cores(mid)
    mid_beyond = exchange("gx", *mid_faces[:2]) + exchange("gy", *mid_faces[2:])
    part, gather_map = run(
        functools.partial(second_inner_kernel, cap),
        [cells, shaped(slots, cx * cy, dtype=bf16)],
        mid,
        mid0,
        pressure,
        buoyancy,
        kappa,
        other_mid,
        other_b,
        got,
        flops=100 * cx * cy * cz,
        scratch=scratch,
    )
    pressure_next, picked = run(
        second_edge_kernel,
        [pltpu.VMEM((cx, cy, cz), f32), pltpu.VMEM((groups, cap, lanes), f32)],
        part,
        mid,
        buoyancy,
        kappa,
        bx,
        by,
        gather_map,
        *mid_beyond,
        flops=6 * slots * cx * cy * lanes,
    )
    returned = exchange_rows(picked, orders)
    hull_pressure, pressure_next = run(
        unpack_kernel,
        [shaped(rows, lanes), cells],
        unpack_map,
        returned,
        pressure_next,
        out_space=pl.ANY,
        flops=4 * rows * slots * lanes,
        scratch=[pltpu.VMEM((rows, lanes), f32), pltpu.SemaphoreType.DMA((3,))],
    )
    return pressure_next, hull_pressure


def solution(mesh):
    cells = P("gx", "gy", "blk")
    rows = P(("gx", "gy", "blk"), None)
    return jax.shard_map(
        local,
        mesh=mesh,
        in_specs=(cells, cells, cells, cells, rows, rows, rows),
        out_specs=(cells, rows),
        check_vma=False,
    )
```

```python
import functools
import math

import jax
import jax.numpy as jnp
import numpy as np
from jax import lax
from jax.experimental import pallas as pl
from jax.experimental.pallas import tpu as pltpu
from jax.sharding import PartitionSpec as P

courant_sq = 0.05
source_gain = 0.5
lap_scale = courant_sq * 0.5 / (24.0 * 24.0)
halo = 3
tile = 8
f32 = jnp.float32
bf16 = jnp.bfloat16
VMEM_LIMIT = 16 << 20
early = 10**11
order_seeds = ((183, 183), (150, 205))


def run(kernel, outs, *args, flops=0, scratch=(), in_space=pltpu.VMEM, out_space=pltpu.VMEM):
    size = sum(4 * math.prod(a.shape) for a in (*args, *outs))
    return pl.pallas_call(
        kernel,
        out_shape=outs,
        in_specs=[pl.BlockSpec(memory_space=in_space)] * len(args),
        out_specs=[
            pl.BlockSpec(memory_space=m) for m in (out_space if isinstance(out_space, list) else [out_space] * len(outs))
        ],
        scratch_shapes=list(scratch),
        compiler_params=pltpu.CompilerParams(vmem_limit_bytes=VMEM_LIMIT),
        cost_estimate=pl.CostEstimate(flops=flops, bytes_accessed=size, transcendentals=0),
    )(*args)


def shaped(*shape, dtype=f32):
    return jax.ShapeDtypeStruct(shape, dtype)


def dot(a, b, contract=((1,), (0,))):
    return lax.dot_general(a, b, (contract, ((), ())), preferred_element_type=f32)


def parts_of(x):
    high = x.astype(bf16)
    return jnp.concatenate([high, (x - high.astype(f32)).astype(bf16)], axis=1)


def select_rows(one_hot, x):
    lanes = x.shape[1]
    y = dot(one_hot, parts_of(x))
    return y[:, :lanes] + y[:, lanes:]


def one_hot_of(index, shape, dim):
    short = jnp.int16
    places = lax.broadcasted_iota(jnp.int32, shape, dim).astype(short)
    return jnp.where(places == index.astype(short), bf16(1), bf16(0))


def as_column(row):
    n = row.shape[1]
    diagonal = lax.broadcasted_iota(jnp.int32, (n, n), 0) == lax.broadcasted_iota(jnp.int32, (n, n), 1)
    return jnp.sum(jnp.where(diagonal, row, 0.0), axis=1, keepdims=True)


def block_orders(groups):
    return [
        [[int(g) for g in np.random.default_rng(seed).permutation(groups)] for seed in seeds] for seeds in order_seeds
    ]


def of_core(first, second):
    return jnp.where(lax.axis_index("blk") == 0, first, second)


def find_blocks(orders, block, rank):
    held = jnp.zeros((rank.shape[0], 1), jnp.int32)
    for at, pair in enumerate(zip(*orders)):
        held = jnp.where(rank[:, :1] == at, of_core(*pair), held)
    named = held == block
    return named, jnp.sum(jnp.where(named, rank, 0), axis=0, keepdims=True)


def exchange_rows(x, orders):
    num_blk = lax.axis_size("blk")
    members = [[g * num_blk + b for g in orders[b]] for b in range(num_blk)]
    return lax.all_to_all(
        x, ("gx", "gy", "blk"), split_axis=0, concat_axis=0, tiled=True, axis_index_groups=members
    )


def slot_kernel(
    out_orders, back_orders, cap, block_hbm, column_hbm, accel_hbm, p_hbm, b_hbm,
    place_ref, back_ref, columns_ref, accel_ref, xe_ref, xo_ref, block_ref, column_ref, sems,
):
    cx, even = p_hbm.shape[0], even_at("gx")
    moves = [(block_hbm, block_ref), (column_hbm, column_ref), (accel_hbm, accel_ref)]
    for field, width, at in ((p_hbm, halo, 0), (b_hbm, 2, halo)):
        moves.append((field.at[pl.ds(jnp.where(even, cx - width, 0), width)], xe_ref.at[pl.ds(at, width)]))
        moves.append((field.at[pl.ds(jnp.where(even, 0, cx - width), width)], xo_ref.at[pl.ds(at, width)]))
    copies = [pltpu.make_async_copy(src, dst, sems.at[i]) for i, (src, dst) in enumerate(moves)]
    for copy in copies:
        copy.start()
    rows, lanes = accel_ref.shape
    before = lax.broadcasted_iota(jnp.int32, (rows, rows), 0) < lax.broadcasted_iota(jnp.int32, (rows, rows), 1)
    before = jnp.where(before, 1.0, 0.0).astype(bf16)
    copies[0].wait()
    copies[1].wait()
    block = block_ref[...]
    column = column_ref[...] + 1
    groups = len(out_orders[0])
    rank = lax.broadcasted_iota(jnp.int32, (groups, rows), 0)
    named, out_at = find_blocks(out_orders, block, rank)
    _, back_at = find_blocks(back_orders, block, rank)
    matches = jnp.where(named, 1.0, 0.0).astype(bf16)
    earlier = dot(matches, before)
    slot = jnp.sum(jnp.where(named, earlier, 0.0), axis=0, keepdims=True).astype(jnp.int32)
    place_ref[...] = out_at * (cap + 1) + slot
    back_ref[...] = (back_at * cap + slot).astype(f32)
    at_slot = lax.broadcasted_iota(jnp.int32, (lanes, rows), 0) % cap == slot
    high = jnp.where(at_slot, column // 32, 0).astype(f32).astype(bf16)
    low = jnp.where(at_slot, column % 32, 0).astype(f32).astype(bf16)
    columns_ref[...] = dot(matches, high, ((1,), (1,))) * 32.0 + dot(matches, low, ((1,), (1,)))
    for copy in copies[2:]:
        copy.wait()


def pack_kernel(cap, place_ref, back_ref, columns_ref, accel_ref, out_hbm, slot_ref, out_ref, sems):
    rows, lanes = accel_ref.shape
    stride = cap + 1
    total = out_ref.shape[0]
    chunks = sems.shape[0]
    chunk = total // chunks
    place = place_ref[...]
    parts = parts_of(accel_ref[...])
    copies = []
    for k in range(chunks):
        part = pl.ds(k * chunk, chunk)
        y = dot(one_hot_of(place - k * chunk, (chunk, rows), 0), parts)
        out_ref[part, :] = y[:, :lanes] + y[:, lanes:]
        for at in range(k * chunk, (k + 1) * chunk):
            if at % stride == cap:
                out_ref[at : at + 1, :] = columns_ref[at // stride : at // stride + 1, :]
        copies.append(pltpu.make_async_copy(out_ref.at[part], out_hbm.at[part], sems.at[k]))
        copies[k].start()
    slot_ref[...] = back_ref[...]
    for copy in copies:
        copy.wait()


def column_rows(got_ref, cap, blocks):
    lanes = got_ref.shape[1]
    stride = cap + 1
    per = lanes // cap
    lane = lax.broadcasted_iota(jnp.int32, (1, lanes), 1) // cap
    rows = []
    for g in range(0, len(blocks), per):
        parts = [got_ref[pl.ds(at * stride + cap, 1), :] for at in blocks[g : g + per]]
        row = parts[0]
        for k in range(1, per):
            row = jnp.where(lane == k, parts[k], row)
        rows.append(row - 1.0)
    return rows


def mid_kernel(cap, got_ref, mid0_ref, kappa_ref, mid_ref, xe_ref, xo_ref, ye_ref, yo_ref, spread_ref, rows_ref):
    lanes = got_ref.shape[1]
    groups = got_ref.shape[0] // (cap + 1)
    cx, cy, cz = mid0_ref.shape
    for at, row in enumerate(column_rows(got_ref, cap, range(groups))):
        spread_ref[:, at * lanes : (at + 1) * lanes] = one_hot_of(row.astype(jnp.int32), (cx * cy, lanes), 0)
    for g in range(groups):
        rows_ref[g * cap : (g + 1) * cap, :] = got_ref[g * (cap + 1) : (g + 1) * (cap + 1) - 1, :]
    source = select_rows(spread_ref[...], rows_ref[...]).reshape(cx, cy, cz)
    mid_ref[...] = mid0_ref[...] + kappa_ref[...] * (source_gain * source)
    send_planes(mid_ref, halo, xe_ref, xo_ref)
    send_rows(((mid_ref, halo),), ye_ref, yo_ref)


def unpack_kernel(map_ref, returned_ref, next_ref, out_hbm, next_hbm, out_ref, sems):
    copies = [pltpu.make_async_copy(next_ref, next_hbm, sems.at[0])]
    copies[0].start()
    rows, slots = map_ref.shape
    lanes = out_ref.shape[1]
    parts = parts_of(returned_ref[...].reshape(slots, lanes))
    half = rows // 2
    for at in (0, half):
        part = pl.ds(at, half)
        y = dot(map_ref[part, :], parts)
        out_ref[part, :] = y[:, :lanes] + y[:, lanes:]
        copies.append(pltpu.make_async_copy(out_ref.at[part], out_hbm.at[part], sems.at[len(copies)]))
        copies[-1].start()
    for copy in copies:
        copy.wait()


def even_at(axis):
    return lax.axis_index(axis) % 2 == 0


def y_row(ref, j):
    cx, cy, cz = ref.shape
    return ref.reshape(cx * cy, cz)[pl.ds(j, cx, stride=cy), :]


def send_planes(ref, width, xe_ref, xo_ref):
    cx, even = ref.shape[0], even_at("gx")
    xe_ref[...] = ref[pl.ds(jnp.where(even, cx - width, 0), width)]
    xo_ref[...] = ref[pl.ds(jnp.where(even, 0, cx - width), width)]


def send_rows(fields, ye_ref, yo_ref):
    at, even = 0, even_at("gy")
    for ref, width in fields:
        cy = ref.shape[1]
        for k in range(width):
            low, high = y_row(ref, k), y_row(ref, cy - width + k)
            ye_ref[at + k] = jnp.where(even, high, low)
            yo_ref[at + k] = jnp.where(even, low, high)
        at += width


def low_and_high(axis, from_even, from_odd):
    at = lax.axis_index(axis)
    even = at % 2 == 0
    low = jnp.where(at > 0, jnp.where(even, from_odd, from_even), 0.0)
    high = jnp.where(at < lax.axis_size(axis) - 1, jnp.where(even, from_even, from_odd), 0.0)
    return low, high


def swap_pairs(sizes, axis, first):
    num_gx, num_gy, num_blk = sizes
    pairs = []
    for x in range(num_gx):
        for y in range(num_gy):
            for b in range(num_blk):
                at, count = (x, num_gx) if axis == "gx" else (y, num_gy)
                other = at + 1 if at % 2 == first else at - 1
                if 0 <= other < count:
                    to = (other, y, b) if axis == "gx" else (x, other, b)
                else:
                    to = (x, y, num_blk - 1 - b)
                pairs.append(((x * num_gy + y) * num_blk + b, (to[0] * num_gy + to[1]) * num_blk + to[2]))
    return pairs


def exchange(axis, to_even, to_odd):
    axes = ("gx", "gy", "blk")
    sizes = tuple(lax.axis_size(a) for a in axes)
    to_odd = lax.ppermute(to_odd, axes, swap_pairs(sizes, axis, 1))
    return lax.ppermute(to_even, axes, swap_pairs(sizes, axis, 0)), to_odd


def swap_cores(x):
    count = lax.axis_size("blk")
    return lax.ppermute(x, "blk", [(i, count - 1 - i) for i in range(count)])


def row_face_kernel(p_ref, b_ref, slot_ref, xe_ref, xo_ref, ye_ref, yo_ref, p_out_ref, b_out_ref, bx_ref, map_ref):
    cx, _, lanes = p_ref.shape
    send_rows(((p_ref, halo), (b_ref, 2)), ye_ref, yo_ref)
    p_out_ref[...] = p_ref[...]
    b_out_ref[...] = b_ref[...]
    low, high = low_and_high("gx", xe_ref[halo:], xo_ref[halo:])
    bx_ref[0] = low[1] + b_ref[0]
    bx_ref[1] = low[0] + low[1]
    bx_ref[2] = high[0] + b_ref[cx - 1]
    bx_ref[3] = high[0] + high[1]
    rows, slots = map_ref.shape
    for at in range(0, rows, lanes):
        column = as_column(slot_ref[:, at : at + lanes]).astype(jnp.int32)
        map_ref[at : at + lanes, :] = one_hot_of(column, (lanes, slots), 1)


def ahead(x, beyond, lane, step):
    lanes = x.shape[-1]
    if step > 0:
        return pltpu.roll(jnp.where(lane < step, beyond, x), lanes - step, x.ndim - 1)
    return pltpu.roll(jnp.where(lane >= lanes + step, beyond, x), -step, x.ndim - 1)


def diff(a, b, c, d):
    near = (a if b is None else -b if a is None else a - b) * 27.0
    near = near if c is None else near - c
    return near if d is None else near + d


def inner(v_ref, b_ref, vo_ref, bo_ref, vpad_ref, bpad_ref, fx_ref, fy_ref, finish):
    cx, cy, cz = v_ref.shape
    lane = lax.broadcasted_iota(jnp.int32, (cy, cz), 1)
    last = lax.broadcasted_iota(jnp.int32, (cy, cz), 0) == cy - 1
    start = jnp.where(lax.axis_index("blk") == 0, 0, cz - halo)
    near = (lane >= start) & (lane < start + halo)
    for ref in (vpad_ref, bpad_ref, fy_ref):
        ref[:, :tile] = jnp.zeros((ref.shape[0], tile, cz), f32)
        ref[:, tile + cy :] = jnp.zeros((ref.shape[0], tile, cz), f32)
    vpad_ref[:, tile : tile + cy] = v_ref[...]
    bpad_ref[:, tile : tile + cy] = b_ref[...]

    def plane(ref, i, count):
        return ref[i] if 0 <= i < count else None

    for i in range(cx - 1):
        v = [plane(v_ref, i + k, cx) for k in (-1, 0, 1, 2)]
        fx_ref[i] = diff(v[2], v[1], v[3], v[0]) * (b_ref[i] + b_ref[i + 1])
    for i in range(cx):
        f = [plane(fx_ref, i + k, cx - 1) for k in (-2, -1, 0, 1)]
        total = diff(f[2], f[1], f[3], f[0])
        v = [vpad_ref[i, tile + k : tile + k + cy, :] for k in (-1, 0, 1, 2)]
        b = jnp.where(last, 0.0, b_ref[i] + bpad_ref[i, tile + 1 : tile + 1 + cy, :])
        fy = diff(v[2], v[1], v[3], v[0]) * b
        fy_ref[i % 2, tile : tile + cy, :] = fy
        f = [fy_ref[i % 2, tile + k : tile + k + cy, :] for k in (-2, -1, 1)]
        total += diff(fy, f[1], f[2], f[0])
        u, h = v_ref[i], jnp.where(near, vo_ref[i], 0.0)
        bu, bh = b_ref[i], jnp.where(near, bo_ref[i], 0.0)
        fu = diff(ahead(u, h, lane, 1), u, ahead(u, h, lane, 2), ahead(u, h, lane, -1)) * (bu + ahead(bu, bh, lane, 1))
        fh = diff(ahead(h, u, lane, 1), h, ahead(h, u, lane, 2), ahead(h, u, lane, -1)) * (bh + ahead(bh, bu, lane, 1))
        total += diff(fu, ahead(fu, fh, lane, -1), ahead(fu, fh, lane, 1), ahead(fu, fh, lane, -2))
        finish(i, u, total)


def edge(v0, v1, w1, w2, w3, b0, b1, b3):
    f3 = diff(w1, w2, v0, w3) * b3
    f1 = diff(v0, w1, v1, w2) * b1
    d0 = w1 * b0
    return 27.0 * (d0 - f1) + f3, f1 - 27.0 * d0, d0


def add_edges(out_ref, v_ref, b_ref, kappa_ref, low_x, high_x, low_y, high_y, bx, by):
    cx, cy, cz = v_ref.shape
    flat_out = out_ref.reshape(cx * cy, cz)
    sides = ((low_x, low_y, 0, 1, 0), (high_x, high_y, -1, -1, 2))
    for x, y, first, step, at in sides:
        w = (x[0], x[1], x[2])[:: -step]
        i = first % cx
        terms = edge(v_ref[i], v_ref[i + step], *w, b_ref[i] + b_ref[i + step], bx[at], bx[at + 1])
        for k, term in enumerate(terms):
            out_ref[i + k * step] += kappa_ref[i + k * step] * (lap_scale * term)
    for x, y, first, step, at in sides:
        w = (y[0], y[1], y[2])[:: -step]
        j = first % cy
        v0, v1, b = y_row(v_ref, j), y_row(v_ref, j + step), y_row(b_ref, j) + y_row(b_ref, j + step)
        terms = edge(v0, v1, *w, b, by[at], by[at + 1])
        for k, term in enumerate(terms):
            to = pl.ds(j + k * step, cx, stride=cy)
            flat_out[to, :] = flat_out[to, :] + y_row(kappa_ref, j + k * step) * (lap_scale * term)


def first_inner_kernel(p_ref, b_ref, prev_ref, kappa_ref, po_ref, bo_ref, out_ref, *scratch):
    def finish(i, u, total):
        out_ref[i] = 2.0 * u - prev_ref[i] + kappa_ref[i] * (lap_scale * total)

    inner(p_ref, b_ref, po_ref, bo_ref, *scratch, finish)


def first_edge_kernel(part_ref, p_ref, b_ref, kappa_ref, bx_ref, xe_ref, xo_ref, ye_ref, yo_ref, mid0_ref, by_ref):
    cy = p_ref.shape[1]
    low_x, high_x = low_and_high("gx", xe_ref[:halo], xo_ref[:halo])
    low_y, high_y = low_and_high("gy", ye_ref[...], yo_ref[...])
    by_ref[0] = low_y[4] + y_row(b_ref, 0)
    by_ref[1] = low_y[3] + low_y[4]
    by_ref[2] = high_y[3] + y_row(b_ref, cy - 1)
    by_ref[3] = high_y[3] + high_y[4]
    mid0_ref[...] = part_ref[...]
    add_edges(mid0_ref, p_ref, b_ref, kappa_ref, low_x, high_x, low_y, high_y, bx_ref, by_ref)


def second_inner_kernel(
    out_orders, back_orders, cap, mid_ref, mid0_ref, p_ref, b_ref, kappa_ref, mo_ref, bo_ref, got_ref, out_ref, map_ref, *scratch
):
    cx, cy, _ = p_ref.shape
    lanes = got_ref.shape[1]

    def finish(i, u, total):
        out_ref[i] = 3.0 * u - mid0_ref[i] - p_ref[i] + kappa_ref[i] * (lap_scale * total)

    inner(mid_ref, b_ref, mo_ref, bo_ref, *scratch, finish)
    blocks = [of_core(*(o.index(b[k]) for o, b in zip(out_orders, back_orders))) for k in range(len(out_orders[0]))]
    for at, row in enumerate(column_rows(got_ref, cap, blocks)):
        column = as_column(row).astype(jnp.int32)
        map_ref[at * lanes : (at + 1) * lanes, :] = one_hot_of(column, (lanes, cx * cy), 1)


def second_edge_kernel(
    part_ref, mid_ref, b_ref, kappa_ref, bx_ref, by_ref, map_ref, xe_ref, xo_ref, ye_ref, yo_ref, next_ref, picked_ref
):
    cx, cy, cz = mid_ref.shape
    low_x, high_x = low_and_high("gx", xe_ref[...], xo_ref[...])
    low_y, high_y = low_and_high("gy", ye_ref[...], yo_ref[...])
    next_ref[...] = part_ref[...]
    add_edges(next_ref, mid_ref, b_ref, kappa_ref, low_x, high_x, low_y, high_y, bx_ref, by_ref)
    picked_ref[...] = select_rows(map_ref[...], next_ref[...].reshape(cx * cy, cz)).reshape(picked_ref.shape)


def local(pressure, pressure_prev, buoyancy, kappa, hull_accel, row_block, row_column):
    groups = lax.axis_size("gx") * lax.axis_size("gy")
    orders = block_orders(groups)
    rows, lanes = hull_accel.shape
    cap = 2 * rows // groups
    cx, cy, cz = pressure.shape
    slots, stride = groups * cap, cap + 1
    cells = shaped(cx, cy, cz)

    in_hbm = [pltpu.with_memory_space_constraint(a, pltpu.HBM) for a in (
        row_block.reshape(1, rows), row_column.reshape(1, rows), hull_accel, pressure, buoyancy)]
    place, back, columns, accel, xe, xo = run(
        functools.partial(slot_kernel, *orders, cap),
        [shaped(1, rows, dtype=jnp.int32), shaped(1, rows), shaped(groups, lanes)] + [pltpu.VMEM(o, f32) for o in ((rows, lanes),) + ((halo + 2, cy, cz),) * 2],
        *in_hbm,
        in_space=pl.ANY,
        flops=2 * groups * rows * rows,
        scratch=[pltpu.VMEM((1, rows), jnp.int32)] * 2 + [pltpu.SemaphoreType.DMA((7,))],
    )
    chunks = max(n for n in range(1, 6) if groups * stride % (n * tile) == 0)
    outgoing, slot = run(
        functools.partial(pack_kernel, cap),
        [shaped(groups * stride, lanes), shaped(1, rows)],
        place,
        back,
        columns,
        accel,
        out_space=[pl.ANY, pltpu.VMEM],
        flops=4 * groups * stride * rows * lanes,
        scratch=[pltpu.VMEM((groups * stride, lanes), f32), pltpu.SemaphoreType.DMA((chunks,))],
    )
    got = exchange_rows(outgoing.reshape(groups, stride, 1, lanes), orders[0]).reshape(groups * stride, lanes)

    xe, xo = exchange("gx", xe, xo)
    ye, yo, p_out, b_out, bx, unpack_map = run(
        row_face_kernel,
        [shaped(halo + 2, cx, cz)] * 2 + [cells] * 2 + [shaped(4, cy, cz), shaped(rows, slots, dtype=bf16)],
        pressure,
        buoyancy,
        slot,
        xe,
        xo,
        flops=early,
    )
    other_b = swap_cores(b_out)
    ye, yo = exchange("gy", ye, yo)
    scratch = [pltpu.VMEM((cx, cy + 2 * tile, cz), f32)] * 2 + [
        pltpu.VMEM((cx, cy, cz), f32),
        pltpu.VMEM((2, cy + 2 * tile, cz), f32),
    ]
    (part,) = run(
        first_inner_kernel,
        [cells],
        pressure,
        buoyancy,
        pressure_prev,
        kappa,
        swap_cores(p_out),
        other_b,
        flops=100 * cx * cy * cz,
        scratch=scratch,
    )
    mid0, by = run(
        first_edge_kernel, [cells, shaped(4, cx, cz)], part, pressure, buoyancy, kappa, bx, xe, xo, ye, yo
    )

    mid, *mid_faces = run(
        functools.partial(mid_kernel, cap),
        [cells] + [shaped(halo, cy, cz)] * 2 + [shaped(halo, cx, cz)] * 2,
        got,
        mid0,
        kappa,
        flops=6 * cx * cy * slots * lanes,
        scratch=[pltpu.VMEM((cx * cy, slots), bf16), pltpu.VMEM((slots, lanes), f32)],
    )
    other_mid = swap_cores(mid)
    mid_beyond = exchange("gx", *mid_faces[:2]) + exchange("gy", *mid_faces[2:])
    part, gather_map = run(
        functools.partial(second_inner_kernel, *orders, cap),
        [cells, shaped(slots, cx * cy, dtype=bf16)],
        mid,
        mid0,
        pressure,
        buoyancy,
        kappa,
        other_mid,
        other_b,
        got,
        flops=100 * cx * cy * cz,
        scratch=scratch,
    )
    pressure_next, picked = run(
        second_edge_kernel,
        [pltpu.VMEM((cx, cy, cz), f32), pltpu.VMEM((groups, cap, lanes), f32)],
        part,
        mid,
        buoyancy,
        kappa,
        bx,
        by,
        gather_map,
        *mid_beyond,
        flops=6 * slots * cx * cy * lanes,
    )
    returned = exchange_rows(picked, orders[1])
    hull_pressure, pressure_next = run(
        unpack_kernel,
        [shaped(rows, lanes), cells],
        unpack_map,
        returned,
        pressure_next,
        out_space=pl.ANY,
        flops=4 * rows * slots * lanes,
        scratch=[pltpu.VMEM((rows, lanes), f32), pltpu.SemaphoreType.DMA((3,))],
    )
    return pressure_next, hull_pressure


def solution(mesh):
    cells = P("gx", "gy", "blk")
    rows = P(("gx", "gy", "blk"), None)
    return jax.shard_map(
        local,
        mesh=mesh,
        in_specs=(cells, cells, cells, cells, rows, rows, rows),
        out_specs=(cells, rows),
        check_vma=False,
    )
```

```python
import functools
import math

import jax
import jax.numpy as jnp
import numpy as np
from jax import lax
from jax.experimental import pallas as pl
from jax.experimental.pallas import tpu as pltpu
from jax.sharding import PartitionSpec as P

courant_sq = 0.05
source_gain = 0.5
lap_scale = courant_sq * 0.5 / (24.0 * 24.0)
halo = 3
tile = 8
f32 = jnp.float32
bf16 = jnp.bfloat16
VMEM_LIMIT = 16 << 20
early = 10**11
order_seeds = ((183, 183), (150, 205))


def run(kernel, outs, *args, flops=0, scratch=(), in_space=pltpu.VMEM, out_space=pltpu.VMEM):
    size = sum(4 * math.prod(a.shape) for a in (*args, *outs))
    return pl.pallas_call(
        kernel,
        out_shape=outs,
        in_specs=[pl.BlockSpec(memory_space=in_space)] * len(args),
        out_specs=[
            pl.BlockSpec(memory_space=m) for m in (out_space if isinstance(out_space, list) else [out_space] * len(outs))
        ],
        scratch_shapes=list(scratch),
        compiler_params=pltpu.CompilerParams(vmem_limit_bytes=VMEM_LIMIT),
        cost_estimate=pl.CostEstimate(flops=flops, bytes_accessed=size, transcendentals=0),
    )(*args)


def shaped(*shape, dtype=f32):
    return jax.ShapeDtypeStruct(shape, dtype)


def dot(a, b, contract=((1,), (0,))):
    return lax.dot_general(a, b, (contract, ((), ())), preferred_element_type=f32)


def parts_of(x):
    high = x.astype(bf16)
    return jnp.concatenate([high, (x - high.astype(f32)).astype(bf16)], axis=1)


def select_rows(one_hot, x):
    lanes = x.shape[1]
    y = dot(one_hot, parts_of(x))
    return y[:, :lanes] + y[:, lanes:]


def one_hot_of(index, shape, dim):
    short = jnp.int16
    places = lax.broadcasted_iota(jnp.int32, shape, dim).astype(short)
    return jnp.where(places == index.astype(short), bf16(1), bf16(0))


def as_column(row):
    n = row.shape[1]
    diagonal = lax.broadcasted_iota(jnp.int32, (n, n), 0) == lax.broadcasted_iota(jnp.int32, (n, n), 1)
    return jnp.sum(jnp.where(diagonal, row, 0.0), axis=1, keepdims=True)


def block_orders(groups):
    return [
        [[int(g) for g in np.random.default_rng(seed).permutation(groups)] for seed in seeds] for seeds in order_seeds
    ]


def of_core(first, second):
    return jnp.where(lax.axis_index("blk") == 0, first, second)


def find_blocks(orders, block, rank):
    held = jnp.zeros((rank.shape[0], 1), jnp.int32)
    for at, pair in enumerate(zip(*orders)):
        held = jnp.where(rank[:, :1] == at, of_core(*pair), held)
    named = held == block
    return named, jnp.sum(jnp.where(named, rank, 0), axis=0, keepdims=True)


def exchange_rows(x, orders):
    num_blk = lax.axis_size("blk")
    members = [[g * num_blk + b for g in orders[b]] for b in range(num_blk)]
    return lax.all_to_all(
        x, ("gx", "gy", "blk"), split_axis=0, concat_axis=0, tiled=True, axis_index_groups=members
    )


def slot_kernel(
    out_orders, back_orders, cap, block_hbm, column_hbm, accel_hbm, p_hbm, b_hbm,
    place_ref, back_ref, columns_ref, accel_ref, xe_ref, xo_ref, block_ref, column_ref, sems,
):
    cx, even = p_hbm.shape[0], even_at("gx")
    moves = [(block_hbm, block_ref), (column_hbm, column_ref), (accel_hbm, accel_ref)]
    for field, width, at in ((p_hbm, halo, 0), (b_hbm, 2, halo)):
        moves.append((field.at[pl.ds(jnp.where(even, cx - width, 0), width)], xe_ref.at[pl.ds(at, width)]))
        moves.append((field.at[pl.ds(jnp.where(even, 0, cx - width), width)], xo_ref.at[pl.ds(at, width)]))
    copies = [pltpu.make_async_copy(src, dst, sems.at[i]) for i, (src, dst) in enumerate(moves)]
    for copy in copies:
        copy.start()
    rows, lanes = accel_ref.shape
    before = lax.broadcasted_iota(jnp.int32, (rows, rows), 0) < lax.broadcasted_iota(jnp.int32, (rows, rows), 1)
    before = jnp.where(before, 1.0, 0.0).astype(bf16)
    copies[0].wait()
    copies[1].wait()
    block = block_ref[...]
    column = column_ref[...] + 1
    groups = len(out_orders[0])
    rank = lax.broadcasted_iota(jnp.int32, (groups, rows), 0)
    named, out_at = find_blocks(out_orders, block, rank)
    _, back_at = find_blocks(back_orders, block, rank)
    matches = jnp.where(named, 1.0, 0.0).astype(bf16)
    earlier = dot(matches, before)
    slot = jnp.sum(jnp.where(named, earlier, 0.0), axis=0, keepdims=True).astype(jnp.int32)
    place_ref[...] = out_at * (cap + 1) + slot
    back_ref[...] = (back_at * cap + slot).astype(f32)
    at_slot = lax.broadcasted_iota(jnp.int32, (lanes, rows), 0) % cap == slot
    high = jnp.where(at_slot, column // 32, 0).astype(f32).astype(bf16)
    low = jnp.where(at_slot, column % 32, 0).astype(f32).astype(bf16)
    columns_ref[...] = dot(matches, high, ((1,), (1,))) * 32.0 + dot(matches, low, ((1,), (1,)))
    for copy in copies[2:]:
        copy.wait()


def pack_kernel(cap, place_ref, back_ref, columns_ref, accel_ref, out_hbm, slot_ref, out_ref, sems):
    rows, lanes = accel_ref.shape
    stride = cap + 1
    total = out_ref.shape[0]
    chunks = sems.shape[0]
    chunk = total // chunks
    place = place_ref[...]
    parts = parts_of(accel_ref[...])
    copies = []
    for k in range(chunks):
        part = pl.ds(k * chunk, chunk)
        y = dot(one_hot_of(place - k * chunk, (chunk, rows), 0), parts)
        out_ref[part, :] = y[:, :lanes] + y[:, lanes:]
        for at in range(k * chunk, (k + 1) * chunk):
            if at % stride == cap:
                out_ref[at : at + 1, :] = columns_ref[at // stride : at // stride + 1, :]
        copies.append(pltpu.make_async_copy(out_ref.at[part], out_hbm.at[part], sems.at[k]))
        copies[k].start()
    slot_ref[...] = back_ref[...]
    for copy in copies:
        copy.wait()


def column_rows(got_ref, cap, blocks):
    lanes = got_ref.shape[1]
    stride = cap + 1
    per = lanes // cap
    lane = lax.broadcasted_iota(jnp.int32, (1, lanes), 1) // cap
    rows = []
    for g in range(0, len(blocks), per):
        parts = [got_ref[pl.ds(at * stride + cap, 1), :] for at in blocks[g : g + per]]
        row = parts[0]
        for k in range(1, per):
            row = jnp.where(lane == k, parts[k], row)
        rows.append(row - 1.0)
    return rows


def mid_kernel(cap, got_ref, mid0_ref, kappa_ref, mid_ref, xe_ref, xo_ref, ye_ref, yo_ref, spread_ref, rows_ref):
    lanes = got_ref.shape[1]
    groups = got_ref.shape[0] // (cap + 1)
    cx, cy, cz = mid0_ref.shape
    for at, row in enumerate(column_rows(got_ref, cap, range(groups))):
        spread_ref[:, at * lanes : (at + 1) * lanes] = one_hot_of(row.astype(jnp.int32), (cx * cy, lanes), 0)
    for g in range(groups):
        rows_ref[g * cap : (g + 1) * cap, :] = got_ref[g * (cap + 1) : (g + 1) * (cap + 1) - 1, :]
    source = select_rows(spread_ref[...], rows_ref[...]).reshape(cx, cy, cz)
    mid_ref[...] = mid0_ref[...] + kappa_ref[...] * (source_gain * source)
    send_planes(mid_ref, halo, xe_ref, xo_ref)
    send_rows(((mid_ref, halo),), ye_ref, yo_ref)


def unpack_kernel(map_ref, returned_ref, next_ref, out_hbm, next_hbm, out_ref, sems):
    copies = [pltpu.make_async_copy(next_ref, next_hbm, sems.at[0])]
    copies[0].start()
    rows, slots = map_ref.shape
    lanes = out_ref.shape[1]
    parts = parts_of(returned_ref[...].reshape(slots, lanes))
    half = rows // 2
    for at in (0, half):
        part = pl.ds(at, half)
        y = dot(map_ref[part, :], parts)
        out_ref[part, :] = y[:, :lanes] + y[:, lanes:]
        copies.append(pltpu.make_async_copy(out_ref.at[part], out_hbm.at[part], sems.at[len(copies)]))
        copies[-1].start()
    for copy in copies:
        copy.wait()


def even_at(axis):
    return lax.axis_index(axis) % 2 == 0


def y_row(ref, j):
    cx, cy, cz = ref.shape
    return ref.reshape(cx * cy, cz)[pl.ds(j, cx, stride=cy), :]


def send_planes(ref, width, xe_ref, xo_ref):
    cx, even = ref.shape[0], even_at("gx")
    xe_ref[...] = ref[pl.ds(jnp.where(even, cx - width, 0), width)]
    xo_ref[...] = ref[pl.ds(jnp.where(even, 0, cx - width), width)]


def send_rows(fields, ye_ref, yo_ref):
    at, even = 0, even_at("gy")
    for ref, width in fields:
        cy = ref.shape[1]
        for k in range(width):
            low, high = y_row(ref, k), y_row(ref, cy - width + k)
            ye_ref[at + k] = jnp.where(even, high, low)
            yo_ref[at + k] = jnp.where(even, low, high)
        at += width


def low_and_high(axis, from_even, from_odd):
    at = lax.axis_index(axis)
    even = at % 2 == 0
    low = jnp.where(at > 0, jnp.where(even, from_odd, from_even), 0.0)
    high = jnp.where(at < lax.axis_size(axis) - 1, jnp.where(even, from_even, from_odd), 0.0)
    return low, high


def swap_pairs(sizes, axis, first):
    num_gx, num_gy, num_blk = sizes
    pairs = []
    for x in range(num_gx):
        for y in range(num_gy):
            for b in range(num_blk):
                at, count = (x, num_gx) if axis == "gx" else (y, num_gy)
                other = at + 1 if at % 2 == first else at - 1
                if 0 <= other < count:
                    to = (other, y, b) if axis == "gx" else (x, other, b)
                else:
                    to = (x, y, num_blk - 1 - b)
                pairs.append(((x * num_gy + y) * num_blk + b, (to[0] * num_gy + to[1]) * num_blk + to[2]))
    return pairs


def exchange(axis, to_even, to_odd):
    axes = ("gx", "gy", "blk")
    sizes = tuple(lax.axis_size(a) for a in axes)
    to_odd = lax.ppermute(to_odd, axes, swap_pairs(sizes, axis, 1))
    return lax.ppermute(to_even, axes, swap_pairs(sizes, axis, 0)), to_odd


def swap_cores(x):
    count = lax.axis_size("blk")
    return lax.ppermute(x, "blk", [(i, count - 1 - i) for i in range(count)])


def row_face_kernel(p_ref, b_ref, slot_ref, xe_ref, xo_ref, ye_ref, yo_ref, p_out_ref, b_out_ref, bx_ref, map_ref):
    cx, _, lanes = p_ref.shape
    send_rows(((p_ref, halo), (b_ref, 2)), ye_ref, yo_ref)
    p_out_ref[...] = p_ref[...]
    b_out_ref[...] = b_ref[...]
    low, high = low_and_high("gx", xe_ref[halo:], xo_ref[halo:])
    bx_ref[0] = low[1] + b_ref[0]
    bx_ref[1] = low[0] + low[1]
    bx_ref[2] = high[0] + b_ref[cx - 1]
    bx_ref[3] = high[0] + high[1]
    rows, slots = map_ref.shape
    for at in range(0, rows, lanes):
        column = as_column(slot_ref[:, at : at + lanes]).astype(jnp.int32)
        map_ref[at : at + lanes, :] = one_hot_of(column, (lanes, slots), 1)


def ahead(x, beyond, lane, step):
    lanes = x.shape[-1]
    if step > 0:
        return pltpu.roll(jnp.where(lane < step, beyond, x), lanes - step, x.ndim - 1)
    return pltpu.roll(jnp.where(lane >= lanes + step, beyond, x), -step, x.ndim - 1)


def diff(a, b, c, d):
    near = (a if b is None else -b if a is None else a - b) * 27.0
    near = near if c is None else near - c
    return near if d is None else near + d


def inner(v_ref, b_ref, vo_ref, bo_ref, bz_ref, first, vpad_ref, bpad_ref, fx_ref, fy_ref, finish):
    cx, cy, cz = v_ref.shape
    lane = lax.broadcasted_iota(jnp.int32, (cy, cz), 1)
    last = lax.broadcasted_iota(jnp.int32, (cy, cz), 0) == cy - 1
    start = jnp.where(lax.axis_index("blk") == 0, 0, cz - halo)
    near = (lane >= start) & (lane < start + halo)
    for ref in (vpad_ref, bpad_ref, fy_ref):
        ref[:, :tile] = jnp.zeros((ref.shape[0], tile, cz), f32)
        ref[:, tile + cy :] = jnp.zeros((ref.shape[0], tile, cz), f32)
    vpad_ref[:, tile : tile + cy] = v_ref[...]
    bpad_ref[:, tile : tile + cy] = b_ref[...]

    def plane(ref, i, count):
        return ref[i] if 0 <= i < count else None

    for i in range(cx - 1):
        v = [plane(v_ref, i + k, cx) for k in (-1, 0, 1, 2)]
        fx_ref[i] = diff(v[2], v[1], v[3], v[0]) * (b_ref[i] + b_ref[i + 1])
    for i in range(cx):
        f = [plane(fx_ref, i + k, cx - 1) for k in (-2, -1, 0, 1)]
        total = diff(f[2], f[1], f[3], f[0])
        v = [vpad_ref[i, tile + k : tile + k + cy, :] for k in (-1, 0, 1, 2)]
        b = jnp.where(last, 0.0, b_ref[i] + bpad_ref[i, tile + 1 : tile + 1 + cy, :])
        fy = diff(v[2], v[1], v[3], v[0]) * b
        fy_ref[i % 2, tile : tile + cy, :] = fy
        f = [fy_ref[i % 2, tile + k : tile + k + cy, :] for k in (-2, -1, 1)]
        total += diff(fy, f[1], f[2], f[0])
        u, h = v_ref[i], jnp.where(near, vo_ref[i], 0.0)
        bu, bh = b_ref[i], jnp.where(near, bo_ref[i], 0.0)
        if first:
            bz_ref[i] = bu + ahead(bu, bh, lane, 1)
        fu = diff(ahead(u, h, lane, 1), u, ahead(u, h, lane, 2), ahead(u, h, lane, -1)) * bz_ref[i]
        fh = diff(ahead(h, u, lane, 1), h, ahead(h, u, lane, 2), ahead(h, u, lane, -1)) * (bh + ahead(bh, bu, lane, 1))
        total += diff(fu, ahead(fu, fh, lane, -1), ahead(fu, fh, lane, 1), ahead(fu, fh, lane, -2))
        finish(i, u, total)


def edge(v0, v1, w1, w2, w3, b0, b1, b3):
    f3 = diff(w1, w2, v0, w3) * b3
    f1 = diff(v0, w1, v1, w2) * b1
    d0 = w1 * b0
    return 27.0 * (d0 - f1) + f3, f1 - 27.0 * d0, d0


def add_edges(out_ref, v_ref, b_ref, kappa_ref, low_x, high_x, low_y, high_y, bx, by):
    cx, cy, cz = v_ref.shape
    flat_out = out_ref.reshape(cx * cy, cz)
    sides = ((low_x, low_y, 0, 1, 0), (high_x, high_y, -1, -1, 2))
    for x, y, first, step, at in sides:
        w = (x[0], x[1], x[2])[:: -step]
        i = first % cx
        terms = edge(v_ref[i], v_ref[i + step], *w, b_ref[i] + b_ref[i + step], bx[at], bx[at + 1])
        for k, term in enumerate(terms):
            out_ref[i + k * step] += kappa_ref[i + k * step] * (lap_scale * term)
    for x, y, first, step, at in sides:
        w = (y[0], y[1], y[2])[:: -step]
        j = first % cy
        v0, v1, b = y_row(v_ref, j), y_row(v_ref, j + step), y_row(b_ref, j) + y_row(b_ref, j + step)
        terms = edge(v0, v1, *w, b, by[at], by[at + 1])
        for k, term in enumerate(terms):
            to = pl.ds(j + k * step, cx, stride=cy)
            flat_out[to, :] = flat_out[to, :] + y_row(kappa_ref, j + k * step) * (lap_scale * term)


def first_inner_kernel(p_ref, b_ref, prev_ref, kappa_ref, po_ref, bo_ref, out_ref, bz_ref, *scratch):
    def finish(i, u, total):
        out_ref[i] = 2.0 * u - prev_ref[i] + kappa_ref[i] * (lap_scale * total)

    inner(p_ref, b_ref, po_ref, bo_ref, bz_ref, True, *scratch, finish)


def first_edge_kernel(part_ref, p_ref, b_ref, kappa_ref, bx_ref, xe_ref, xo_ref, ye_ref, yo_ref, mid0_ref, by_ref):
    cy = p_ref.shape[1]
    low_x, high_x = low_and_high("gx", xe_ref[:halo], xo_ref[:halo])
    low_y, high_y = low_and_high("gy", ye_ref[...], yo_ref[...])
    by_ref[0] = low_y[4] + y_row(b_ref, 0)
    by_ref[1] = low_y[3] + low_y[4]
    by_ref[2] = high_y[3] + y_row(b_ref, cy - 1)
    by_ref[3] = high_y[3] + high_y[4]
    mid0_ref[...] = part_ref[...]
    add_edges(mid0_ref, p_ref, b_ref, kappa_ref, low_x, high_x, low_y, high_y, bx_ref, by_ref)


def second_inner_kernel(
    out_orders, back_orders, cap, mid_ref, mid0_ref, p_ref, b_ref, kappa_ref, mo_ref, bo_ref, bz_ref, got_ref, out_ref, map_ref, *scratch
):
    cx, cy, _ = p_ref.shape
    lanes = got_ref.shape[1]

    def finish(i, u, total):
        out_ref[i] = 3.0 * u - mid0_ref[i] - p_ref[i] + kappa_ref[i] * (lap_scale * total)

    inner(mid_ref, b_ref, mo_ref, bo_ref, bz_ref, False, *scratch, finish)
    blocks = [of_core(*(o.index(b[k]) for o, b in zip(out_orders, back_orders))) for k in range(len(out_orders[0]))]
    for at, row in enumerate(column_rows(got_ref, cap, blocks)):
        column = as_column(row).astype(jnp.int32)
        map_ref[at * lanes : (at + 1) * lanes, :] = one_hot_of(column, (lanes, cx * cy), 1)


def second_edge_kernel(
    part_ref, mid_ref, b_ref, kappa_ref, bx_ref, by_ref, map_ref, xe_ref, xo_ref, ye_ref, yo_ref, next_ref, picked_ref
):
    cx, cy, cz = mid_ref.shape
    low_x, high_x = low_and_high("gx", xe_ref[...], xo_ref[...])
    low_y, high_y = low_and_high("gy", ye_ref[...], yo_ref[...])
    next_ref[...] = part_ref[...]
    add_edges(next_ref, mid_ref, b_ref, kappa_ref, low_x, high_x, low_y, high_y, bx_ref, by_ref)
    picked_ref[...] = select_rows(map_ref[...], next_ref[...].reshape(cx * cy, cz)).reshape(picked_ref.shape)


def local(pressure, pressure_prev, buoyancy, kappa, hull_accel, row_block, row_column):
    groups = lax.axis_size("gx") * lax.axis_size("gy")
    orders = block_orders(groups)
    rows, lanes = hull_accel.shape
    cap = 2 * rows // groups
    cx, cy, cz = pressure.shape
    slots, stride = groups * cap, cap + 1
    cells = shaped(cx, cy, cz)

    in_hbm = [pltpu.with_memory_space_constraint(a, pltpu.HBM) for a in (
        row_block.reshape(1, rows), row_column.reshape(1, rows), hull_accel, pressure, buoyancy)]
    place, back, columns, accel, xe, xo = run(
        functools.partial(slot_kernel, *orders, cap),
        [shaped(1, rows, dtype=jnp.int32), shaped(1, rows), shaped(groups, lanes)] + [pltpu.VMEM(o, f32) for o in ((rows, lanes),) + ((halo + 2, cy, cz),) * 2],
        *in_hbm,
        in_space=pl.ANY,
        flops=2 * groups * rows * rows,
        scratch=[pltpu.VMEM((1, rows), jnp.int32)] * 2 + [pltpu.SemaphoreType.DMA((7,))],
    )
    chunks = max(n for n in range(1, 6) if groups * stride % (n * tile) == 0)
    outgoing, slot = run(
        functools.partial(pack_kernel, cap),
        [shaped(groups * stride, lanes), shaped(1, rows)],
        place,
        back,
        columns,
        accel,
        out_space=[pl.ANY, pltpu.VMEM],
        flops=4 * groups * stride * rows * lanes,
        scratch=[pltpu.VMEM((groups * stride, lanes), f32), pltpu.SemaphoreType.DMA((chunks,))],
    )
    got = exchange_rows(outgoing.reshape(groups, stride, 1, lanes), orders[0]).reshape(groups * stride, lanes)

    xe, xo = exchange("gx", xe, xo)
    ye, yo, p_out, b_out, bx, unpack_map = run(
        row_face_kernel,
        [shaped(halo + 2, cx, cz)] * 2 + [cells] * 2 + [shaped(4, cy, cz), shaped(rows, slots, dtype=bf16)],
        pressure,
        buoyancy,
        slot,
        xe,
        xo,
        flops=early,
    )
    other_b = swap_cores(b_out)
    ye, yo = exchange("gy", ye, yo)
    scratch = [pltpu.VMEM((cx, cy + 2 * tile, cz), f32)] * 2 + [
        pltpu.VMEM((cx, cy, cz), f32),
        pltpu.VMEM((2, cy + 2 * tile, cz), f32),
    ]
    part, bz = run(
        first_inner_kernel,
        [cells, cells],
        pressure,
        buoyancy,
        pressure_prev,
        kappa,
        swap_cores(p_out),
        other_b,
        flops=100 * cx * cy * cz,
        scratch=scratch,
    )
    mid0, by = run(
        first_edge_kernel, [cells, shaped(4, cx, cz)], part, pressure, buoyancy, kappa, bx, xe, xo, ye, yo
    )

    mid, *mid_faces = run(
        functools.partial(mid_kernel, cap),
        [cells] + [shaped(halo, cy, cz)] * 2 + [shaped(halo, cx, cz)] * 2,
        got,
        mid0,
        kappa,
        flops=6 * cx * cy * slots * lanes,
        scratch=[pltpu.VMEM((cx * cy, slots), bf16), pltpu.VMEM((slots, lanes), f32)],
    )
    other_mid = swap_cores(mid)
    mid_beyond = exchange("gx", *mid_faces[:2]) + exchange("gy", *mid_faces[2:])
    part, gather_map = run(
        functools.partial(second_inner_kernel, *orders, cap),
        [cells, shaped(slots, cx * cy, dtype=bf16)],
        mid,
        mid0,
        pressure,
        buoyancy,
        kappa,
        other_mid,
        other_b,
        bz,
        got,
        flops=100 * cx * cy * cz,
        scratch=scratch,
    )
    pressure_next, picked = run(
        second_edge_kernel,
        [pltpu.VMEM((cx, cy, cz), f32), pltpu.VMEM((groups, cap, lanes), f32)],
        part,
        mid,
        buoyancy,
        kappa,
        bx,
        by,
        gather_map,
        *mid_beyond,
        flops=6 * slots * cx * cy * lanes,
    )
    returned = exchange_rows(picked, orders[1])
    hull_pressure, pressure_next = run(
        unpack_kernel,
        [shaped(rows, lanes), cells],
        unpack_map,
        returned,
        pressure_next,
        out_space=pl.ANY,
        flops=4 * rows * slots * lanes,
        scratch=[pltpu.VMEM((rows, lanes), f32), pltpu.SemaphoreType.DMA((3,))],
    )
    return pressure_next, hull_pressure


def solution(mesh):
    cells = P("gx", "gy", "blk")
    rows = P(("gx", "gy", "blk"), None)
    return jax.shard_map(
        local,
        mesh=mesh,
        in_specs=(cells, cells, cells, cells, rows, rows, rows),
        out_specs=(cells, rows),
        check_vma=False,
    )
```

```python
import functools
import math

import jax
import jax.numpy as jnp
import numpy as np
from jax import lax
from jax.experimental import pallas as pl
from jax.experimental.pallas import tpu as pltpu
from jax.sharding import PartitionSpec as P

courant_sq = 0.05
source_gain = 0.5
lap_scale = courant_sq * 0.5 / (24.0 * 24.0)
halo = 3
tile = 8
f32 = jnp.float32
bf16 = jnp.bfloat16
VMEM_LIMIT = 16 << 20
early = 10**11
order_seeds = ((183, 183), (150, 205))


def run(kernel, outs, *args, flops=0, scratch=(), in_space=pltpu.VMEM, out_space=pltpu.VMEM):
    size = sum(4 * math.prod(a.shape) for a in (*args, *outs))
    return pl.pallas_call(
        kernel,
        out_shape=outs,
        in_specs=[
            pl.BlockSpec(memory_space=m) for m in (in_space if isinstance(in_space, list) else [in_space] * len(args))
        ],
        out_specs=[
            pl.BlockSpec(memory_space=m) for m in (out_space if isinstance(out_space, list) else [out_space] * len(outs))
        ],
        scratch_shapes=list(scratch),
        compiler_params=pltpu.CompilerParams(vmem_limit_bytes=VMEM_LIMIT),
        cost_estimate=pl.CostEstimate(flops=flops, bytes_accessed=size, transcendentals=0),
    )(*args)


def shaped(*shape, dtype=f32):
    return jax.ShapeDtypeStruct(shape, dtype)


def dot(a, b, contract=((1,), (0,))):
    return lax.dot_general(a, b, (contract, ((), ())), preferred_element_type=f32)


def parts_of(x):
    high = x.astype(bf16)
    return jnp.concatenate([high, (x - high.astype(f32)).astype(bf16)], axis=1)


def select_rows(one_hot, x):
    lanes = x.shape[1]
    y = dot(one_hot, parts_of(x))
    return y[:, :lanes] + y[:, lanes:]


def one_hot_of(index, shape, dim):
    short = jnp.int16
    places = lax.broadcasted_iota(jnp.int32, shape, dim).astype(short)
    return jnp.where(places == index.astype(short), bf16(1), bf16(0))


def as_column(row):
    n = row.shape[1]
    diagonal = lax.broadcasted_iota(jnp.int32, (n, n), 0) == lax.broadcasted_iota(jnp.int32, (n, n), 1)
    return jnp.sum(jnp.where(diagonal, row, 0.0), axis=1, keepdims=True)


def block_orders(groups):
    return [
        [[int(g) for g in np.random.default_rng(seed).permutation(groups)] for seed in seeds] for seeds in order_seeds
    ]


def of_core(first, second):
    return jnp.where(lax.axis_index("blk") == 0, first, second)


def find_blocks(orders, block, rank):
    held = jnp.zeros((rank.shape[0], 1), jnp.int32)
    for at, pair in enumerate(zip(*orders)):
        held = jnp.where(rank[:, :1] == at, of_core(*pair), held)
    named = held == block
    return named, jnp.sum(jnp.where(named, rank, 0), axis=0, keepdims=True)


def exchange_rows(x, orders):
    num_blk = lax.axis_size("blk")
    members = [[g * num_blk + b for g in orders[b]] for b in range(num_blk)]
    return lax.all_to_all(
        x, ("gx", "gy", "blk"), split_axis=0, concat_axis=0, tiled=True, axis_index_groups=members
    )


def slot_kernel(
    out_orders, back_orders, cap, block_hbm, column_hbm, accel_hbm, p_hbm, b_hbm,
    place_ref, back_ref, columns_ref, accel_ref, xe_ref, xo_ref, block_ref, column_ref, sems,
):
    cx, even = p_hbm.shape[0], even_at("gx")
    moves = [(block_hbm, block_ref), (column_hbm, column_ref), (accel_hbm, accel_ref)]
    for field, width, at in ((p_hbm, halo, 0), (b_hbm, 2, halo)):
        moves.append((field.at[pl.ds(jnp.where(even, cx - width, 0), width)], xe_ref.at[pl.ds(at, width)]))
        moves.append((field.at[pl.ds(jnp.where(even, 0, cx - width), width)], xo_ref.at[pl.ds(at, width)]))
    copies = [pltpu.make_async_copy(src, dst, sems.at[i]) for i, (src, dst) in enumerate(moves)]
    for copy in copies:
        copy.start()
    rows, lanes = accel_ref.shape
    before = lax.broadcasted_iota(jnp.int32, (rows, rows), 0) < lax.broadcasted_iota(jnp.int32, (rows, rows), 1)
    before = jnp.where(before, 1.0, 0.0).astype(bf16)
    copies[0].wait()
    copies[1].wait()
    block = block_ref[...]
    column = column_ref[...] + 1
    groups = len(out_orders[0])
    rank = lax.broadcasted_iota(jnp.int32, (groups, rows), 0)
    named, out_at = find_blocks(out_orders, block, rank)
    _, back_at = find_blocks(back_orders, block, rank)
    matches = jnp.where(named, 1.0, 0.0).astype(bf16)
    earlier = dot(matches, before)
    slot = jnp.sum(jnp.where(named, earlier, 0.0), axis=0, keepdims=True).astype(jnp.int32)
    place_ref[...] = out_at * (cap + 1) + slot
    back_ref[...] = (back_at * cap + slot).astype(f32)
    at_slot = lax.broadcasted_iota(jnp.int32, (lanes, rows), 0) % cap == slot
    high = jnp.where(at_slot, column // 32, 0).astype(f32).astype(bf16)
    low = jnp.where(at_slot, column % 32, 0).astype(f32).astype(bf16)
    columns_ref[...] = dot(matches, high, ((1,), (1,))) * 32.0 + dot(matches, low, ((1,), (1,)))
    for copy in copies[2:]:
        copy.wait()


def pack_kernel(cap, place_ref, back_ref, columns_ref, accel_ref, out_hbm, slot_ref, out_ref, sems):
    rows, lanes = accel_ref.shape
    stride = cap + 1
    total = out_ref.shape[0]
    chunks = sems.shape[0]
    chunk = total // chunks
    place = place_ref[...]
    parts = parts_of(accel_ref[...])
    copies = []
    for k in range(chunks):
        part = pl.ds(k * chunk, chunk)
        y = dot(one_hot_of(place - k * chunk, (chunk, rows), 0), parts)
        out_ref[part, :] = y[:, :lanes] + y[:, lanes:]
        for at in range(k * chunk, (k + 1) * chunk):
            if at % stride == cap:
                out_ref[at : at + 1, :] = columns_ref[at // stride : at // stride + 1, :]
        copies.append(pltpu.make_async_copy(out_ref.at[part], out_hbm.at[part], sems.at[k]))
        copies[k].start()
    slot_ref[...] = back_ref[...]
    for copy in copies:
        copy.wait()


def column_rows(got_ref, cap, blocks):
    lanes = got_ref.shape[1]
    stride = cap + 1
    per = lanes // cap
    lane = lax.broadcasted_iota(jnp.int32, (1, lanes), 1) // cap
    rows = []
    for g in range(0, len(blocks), per):
        parts = [got_ref[pl.ds(at * stride + cap, 1), :] for at in blocks[g : g + per]]
        row = parts[0]
        for k in range(1, per):
            row = jnp.where(lane == k, parts[k], row)
        rows.append(row - 1.0)
    return rows


def mid_kernel(cap, got_ref, mid0_ref, kappa_ref, mid_ref, xe_ref, xo_ref, ye_ref, yo_ref, spread_ref, rows_ref):
    lanes = got_ref.shape[1]
    groups = got_ref.shape[0] // (cap + 1)
    cx, cy, cz = mid0_ref.shape
    for at, row in enumerate(column_rows(got_ref, cap, range(groups))):
        spread_ref[:, at * lanes : (at + 1) * lanes] = one_hot_of(row.astype(jnp.int32), (cx * cy, lanes), 0)
    for g in range(groups):
        rows_ref[g * cap : (g + 1) * cap, :] = got_ref[g * (cap + 1) : (g + 1) * (cap + 1) - 1, :]
    source = select_rows(spread_ref[...], rows_ref[...]).reshape(cx, cy, cz)
    mid_ref[...] = mid0_ref[...] + kappa_ref[...] * (source_gain * source)
    send_planes(mid_ref, halo, xe_ref, xo_ref)
    send_rows(((mid_ref, halo),), ye_ref, yo_ref)


def unpack_kernel(map_ref, returned_ref, next_ref, out_hbm, next_hbm, out_ref, sems):
    copies = [pltpu.make_async_copy(next_ref, next_hbm, sems.at[0])]
    copies[0].start()
    rows, slots = map_ref.shape
    lanes = out_ref.shape[1]
    parts = parts_of(returned_ref[...].reshape(slots, lanes))
    half = rows // 2
    for at in (0, half):
        part = pl.ds(at, half)
        y = dot(map_ref[part, :], parts)
        out_ref[part, :] = y[:, :lanes] + y[:, lanes:]
        copies.append(pltpu.make_async_copy(out_ref.at[part], out_hbm.at[part], sems.at[len(copies)]))
        copies[-1].start()
    for copy in copies:
        copy.wait()


def even_at(axis):
    return lax.axis_index(axis) % 2 == 0


def y_row(ref, j):
    cx, cy, cz = ref.shape
    return ref.reshape(cx * cy, cz)[pl.ds(j, cx, stride=cy), :]


def send_planes(ref, width, xe_ref, xo_ref):
    cx, even = ref.shape[0], even_at("gx")
    xe_ref[...] = ref[pl.ds(jnp.where(even, cx - width, 0), width)]
    xo_ref[...] = ref[pl.ds(jnp.where(even, 0, cx - width), width)]


def send_rows(fields, ye_ref, yo_ref):
    at, even = 0, even_at("gy")
    for ref, width in fields:
        cy = ref.shape[1]
        for k in range(width):
            low, high = y_row(ref, k), y_row(ref, cy - width + k)
            ye_ref[at + k] = jnp.where(even, high, low)
            yo_ref[at + k] = jnp.where(even, low, high)
        at += width


def low_and_high(axis, from_even, from_odd):
    at = lax.axis_index(axis)
    even = at % 2 == 0
    low = jnp.where(at > 0, jnp.where(even, from_odd, from_even), 0.0)
    high = jnp.where(at < lax.axis_size(axis) - 1, jnp.where(even, from_even, from_odd), 0.0)
    return low, high


def swap_pairs(sizes, axis, first):
    num_gx, num_gy, num_blk = sizes
    pairs = []
    for x in range(num_gx):
        for y in range(num_gy):
            for b in range(num_blk):
                at, count = (x, num_gx) if axis == "gx" else (y, num_gy)
                other = at + 1 if at % 2 == first else at - 1
                if 0 <= other < count:
                    to = (other, y, b) if axis == "gx" else (x, other, b)
                else:
                    to = (x, y, num_blk - 1 - b)
                pairs.append(((x * num_gy + y) * num_blk + b, (to[0] * num_gy + to[1]) * num_blk + to[2]))
    return pairs


def exchange(axis, to_even, to_odd):
    axes = ("gx", "gy", "blk")
    sizes = tuple(lax.axis_size(a) for a in axes)
    to_odd = lax.ppermute(to_odd, axes, swap_pairs(sizes, axis, 1))
    return lax.ppermute(to_even, axes, swap_pairs(sizes, axis, 0)), to_odd


def swap_cores(x):
    count = lax.axis_size("blk")
    return lax.ppermute(x, "blk", [(i, count - 1 - i) for i in range(count)])


def row_face_kernel(p_ref, b_ref, slot_ref, xe_ref, xo_ref, ye_ref, yo_ref, p_out_ref, b_out_ref, bx_ref, map_ref):
    cx, _, lanes = p_ref.shape
    send_rows(((p_ref, halo), (b_ref, 2)), ye_ref, yo_ref)
    p_out_ref[...] = p_ref[...]
    b_out_ref[...] = b_ref[...]
    low, high = low_and_high("gx", xe_ref[halo:], xo_ref[halo:])
    bx_ref[0] = low[1] + b_ref[0]
    bx_ref[1] = low[0] + low[1]
    bx_ref[2] = high[0] + b_ref[cx - 1]
    bx_ref[3] = high[0] + high[1]
    rows, slots = map_ref.shape
    for at in range(0, rows, lanes):
        column = as_column(slot_ref[:, at : at + lanes]).astype(jnp.int32)
        map_ref[at : at + lanes, :] = one_hot_of(column, (lanes, slots), 1)


def ahead(x, beyond, lane, step):
    lanes = x.shape[-1]
    if step > 0:
        return pltpu.roll(jnp.where(lane < step, beyond, x), lanes - step, x.ndim - 1)
    return pltpu.roll(jnp.where(lane >= lanes + step, beyond, x), -step, x.ndim - 1)


def diff(a, b, c, d):
    near = (a if b is None else -b if a is None else a - b) * 27.0
    near = near if c is None else near - c
    return near if d is None else near + d


def inner(v_ref, b_ref, vo_ref, bo_ref, bz_ref, first, vpad_ref, bpad_ref, fx_ref, fy_ref, finish):
    cx, cy, cz = v_ref.shape
    lane = lax.broadcasted_iota(jnp.int32, (cy, cz), 1)
    last = lax.broadcasted_iota(jnp.int32, (cy, cz), 0) == cy - 1
    start = jnp.where(lax.axis_index("blk") == 0, 0, cz - halo)
    near = (lane >= start) & (lane < start + halo)
    for ref in (vpad_ref, bpad_ref, fy_ref):
        ref[:, :tile] = jnp.zeros((ref.shape[0], tile, cz), f32)
        ref[:, tile + cy :] = jnp.zeros((ref.shape[0], tile, cz), f32)
    vpad_ref[:, tile : tile + cy] = v_ref[...]
    bpad_ref[:, tile : tile + cy] = b_ref[...]

    def plane(ref, i, count):
        return ref[i] if 0 <= i < count else None

    for i in range(cx - 1):
        v = [plane(v_ref, i + k, cx) for k in (-1, 0, 1, 2)]
        fx_ref[i] = diff(v[2], v[1], v[3], v[0]) * (b_ref[i] + b_ref[i + 1])
    for i in range(cx):
        f = [plane(fx_ref, i + k, cx - 1) for k in (-2, -1, 0, 1)]
        total = diff(f[2], f[1], f[3], f[0])
        v = [vpad_ref[i, tile + k : tile + k + cy, :] for k in (-1, 0, 1, 2)]
        b = jnp.where(last, 0.0, b_ref[i] + bpad_ref[i, tile + 1 : tile + 1 + cy, :])
        fy = diff(v[2], v[1], v[3], v[0]) * b
        fy_ref[i % 2, tile : tile + cy, :] = fy
        f = [fy_ref[i % 2, tile + k : tile + k + cy, :] for k in (-2, -1, 1)]
        total += diff(fy, f[1], f[2], f[0])
        u, h = v_ref[i], jnp.where(near, vo_ref[i], 0.0)
        bu, bh = b_ref[i], jnp.where(near, bo_ref[i], 0.0)
        if first:
            bz_ref[i] = bu + ahead(bu, bh, lane, 1)
        fu = diff(ahead(u, h, lane, 1), u, ahead(u, h, lane, 2), ahead(u, h, lane, -1)) * bz_ref[i]
        fh = diff(ahead(h, u, lane, 1), h, ahead(h, u, lane, 2), ahead(h, u, lane, -1)) * (bh + ahead(bh, bu, lane, 1))
        total += diff(fu, ahead(fu, fh, lane, -1), ahead(fu, fh, lane, 1), ahead(fu, fh, lane, -2))
        finish(i, u, total)


def edge(v0, v1, w1, w2, w3, b0, b1, b3):
    f3 = diff(w1, w2, v0, w3) * b3
    f1 = diff(v0, w1, v1, w2) * b1
    d0 = w1 * b0
    return 27.0 * (d0 - f1) + f3, f1 - 27.0 * d0, d0


def add_edges(out_ref, v_ref, b_ref, kappa_ref, low_x, high_x, low_y, high_y, bx, by):
    cx, cy, cz = v_ref.shape
    flat_out = out_ref.reshape(cx * cy, cz)
    sides = ((low_x, low_y, 0, 1, 0), (high_x, high_y, -1, -1, 2))
    for x, y, first, step, at in sides:
        w = (x[0], x[1], x[2])[:: -step]
        i = first % cx
        terms = edge(v_ref[i], v_ref[i + step], *w, b_ref[i] + b_ref[i + step], bx[at], bx[at + 1])
        for k, term in enumerate(terms):
            out_ref[i + k * step] += kappa_ref[i + k * step] * (lap_scale * term)
    for x, y, first, step, at in sides:
        w = (y[0], y[1], y[2])[:: -step]
        j = first % cy
        v0, v1, b = y_row(v_ref, j), y_row(v_ref, j + step), y_row(b_ref, j) + y_row(b_ref, j + step)
        terms = edge(v0, v1, *w, b, by[at], by[at + 1])
        for k, term in enumerate(terms):
            to = pl.ds(j + k * step, cx, stride=cy)
            flat_out[to, :] = flat_out[to, :] + y_row(kappa_ref, j + k * step) * (lap_scale * term)


def first_inner_kernel(p_ref, b_ref, prev_ref, kappa_ref, po_ref, bo_ref, out_ref, bz_ref, *scratch):
    def finish(i, u, total):
        out_ref[i] = 2.0 * u - prev_ref[i] + kappa_ref[i] * (lap_scale * total)

    inner(p_ref, b_ref, po_ref, bo_ref, bz_ref, True, *scratch, finish)


def first_edge_kernel(part_ref, p_ref, b_ref, kappa_ref, bx_ref, xe_ref, xo_ref, ye_ref, yo_ref, mid0_ref, by_ref):
    cy = p_ref.shape[1]
    low_x, high_x = low_and_high("gx", xe_ref[:halo], xo_ref[:halo])
    low_y, high_y = low_and_high("gy", ye_ref[...], yo_ref[...])
    by_ref[0] = low_y[4] + y_row(b_ref, 0)
    by_ref[1] = low_y[3] + low_y[4]
    by_ref[2] = high_y[3] + y_row(b_ref, cy - 1)
    by_ref[3] = high_y[3] + high_y[4]
    mid0_ref[...] = part_ref[...]
    add_edges(mid0_ref, p_ref, b_ref, kappa_ref, low_x, high_x, low_y, high_y, bx_ref, by_ref)


def second_inner_kernel(
    out_orders, back_orders, cap, mid_ref, mid0_ref, p_hbm, b_ref, kappa_ref, mo_ref, bo_ref, bz_ref, got_ref, out_ref, map_ref, p_ref, sem, *scratch
):
    copy = pltpu.make_async_copy(p_hbm, p_ref, sem)
    copy.start()
    cx, cy, _ = p_ref.shape
    lanes = got_ref.shape[1]

    def finish(i, u, total):
        if i == 0:
            copy.wait()
        out_ref[i] = 3.0 * u - mid0_ref[i] - p_ref[i] + kappa_ref[i] * (lap_scale * total)

    inner(mid_ref, b_ref, mo_ref, bo_ref, bz_ref, False, *scratch, finish)
    blocks = [of_core(*(o.index(b[k]) for o, b in zip(out_orders, back_orders))) for k in range(len(out_orders[0]))]
    for at, row in enumerate(column_rows(got_ref, cap, blocks)):
        column = as_column(row).astype(jnp.int32)
        map_ref[at * lanes : (at + 1) * lanes, :] = one_hot_of(column, (lanes, cx * cy), 1)


def second_edge_kernel(
    part_ref, mid_ref, b_ref, kappa_ref, bx_ref, by_ref, map_ref, xe_ref, xo_ref, ye_ref, yo_ref, next_ref, picked_ref
):
    cx, cy, cz = mid_ref.shape
    low_x, high_x = low_and_high("gx", xe_ref[...], xo_ref[...])
    low_y, high_y = low_and_high("gy", ye_ref[...], yo_ref[...])
    next_ref[...] = part_ref[...]
    add_edges(next_ref, mid_ref, b_ref, kappa_ref, low_x, high_x, low_y, high_y, bx_ref, by_ref)
    picked_ref[...] = select_rows(map_ref[...], next_ref[...].reshape(cx * cy, cz)).reshape(picked_ref.shape)


def local(pressure, pressure_prev, buoyancy, kappa, hull_accel, row_block, row_column):
    groups = lax.axis_size("gx") * lax.axis_size("gy")
    orders = block_orders(groups)
    rows, lanes = hull_accel.shape
    cap = 2 * rows // groups
    cx, cy, cz = pressure.shape
    slots, stride = groups * cap, cap + 1
    cells = shaped(cx, cy, cz)

    in_hbm = [pltpu.with_memory_space_constraint(a, pltpu.HBM) for a in (
        row_block.reshape(1, rows), row_column.reshape(1, rows), hull_accel, pressure, buoyancy)]
    place, back, columns, accel, xe, xo = run(
        functools.partial(slot_kernel, *orders, cap),
        [shaped(1, rows, dtype=jnp.int32), shaped(1, rows), shaped(groups, lanes)] + [pltpu.VMEM(o, f32) for o in ((rows, lanes),) + ((halo + 2, cy, cz),) * 2],
        *in_hbm,
        in_space=pl.ANY,
        flops=2 * groups * rows * rows,
        scratch=[pltpu.VMEM((1, rows), jnp.int32)] * 2 + [pltpu.SemaphoreType.DMA((7,))],
    )
    chunks = max(n for n in range(1, 6) if groups * stride % (n * tile) == 0)
    outgoing, slot = run(
        functools.partial(pack_kernel, cap),
        [shaped(groups * stride, lanes), shaped(1, rows)],
        place,
        back,
        columns,
        accel,
        out_space=[pl.ANY, pltpu.VMEM],
        flops=4 * groups * stride * rows * lanes,
        scratch=[pltpu.VMEM((groups * stride, lanes), f32), pltpu.SemaphoreType.DMA((chunks,))],
    )
    got = exchange_rows(outgoing.reshape(groups, stride, 1, lanes), orders[0]).reshape(groups * stride, lanes)

    xe, xo = exchange("gx", xe, xo)
    ye, yo, p_out, b_out, bx, unpack_map = run(
        row_face_kernel,
        [shaped(halo + 2, cx, cz)] * 2 + [cells] * 2 + [shaped(4, cy, cz), shaped(rows, slots, dtype=bf16)],
        pressure,
        buoyancy,
        slot,
        xe,
        xo,
        flops=early,
    )
    other_b = swap_cores(b_out)
    ye, yo = exchange("gy", ye, yo)
    scratch = [pltpu.VMEM((cx, cy + 2 * tile, cz), f32)] * 2 + [
        pltpu.VMEM((cx, cy, cz), f32),
        pltpu.VMEM((2, cy + 2 * tile, cz), f32),
    ]
    part, bz = run(
        first_inner_kernel,
        [cells, cells],
        pressure,
        buoyancy,
        pressure_prev,
        kappa,
        swap_cores(p_out),
        other_b,
        flops=100 * cx * cy * cz,
        scratch=scratch,
    )
    mid0, by = run(
        first_edge_kernel, [cells, shaped(4, cx, cz)], part, pressure, buoyancy, kappa, bx, xe, xo, ye, yo
    )

    mid, *mid_faces = run(
        functools.partial(mid_kernel, cap),
        [cells] + [shaped(halo, cy, cz)] * 2 + [shaped(halo, cx, cz)] * 2,
        got,
        mid0,
        kappa,
        flops=6 * cx * cy * slots * lanes,
        scratch=[pltpu.VMEM((cx * cy, slots), bf16), pltpu.VMEM((slots, lanes), f32)],
    )
    other_mid = swap_cores(mid)
    mid_beyond = exchange("gx", *mid_faces[:2]) + exchange("gy", *mid_faces[2:])
    part, gather_map = run(
        functools.partial(second_inner_kernel, *orders, cap),
        [cells, shaped(slots, cx * cy, dtype=bf16)],
        mid,
        mid0,
        in_hbm[3],
        buoyancy,
        kappa,
        other_mid,
        other_b,
        bz,
        got,
        flops=100 * cx * cy * cz,
        in_space=[pltpu.VMEM] * 2 + [pl.ANY] + [pltpu.VMEM] * 6,
        scratch=[pltpu.VMEM((cx, cy, cz), f32), pltpu.SemaphoreType.DMA] + scratch,
    )
    pressure_next, picked = run(
        second_edge_kernel,
        [pltpu.VMEM((cx, cy, cz), f32), pltpu.VMEM((groups, cap, lanes), f32)],
        part,
        mid,
        buoyancy,
        kappa,
        bx,
        by,
        gather_map,
        *mid_beyond,
        flops=6 * slots * cx * cy * lanes,
    )
    returned = exchange_rows(picked, orders[1])
    hull_pressure, pressure_next = run(
        unpack_kernel,
        [shaped(rows, lanes), cells],
        unpack_map,
        returned,
        pressure_next,
        out_space=pl.ANY,
        flops=4 * rows * slots * lanes,
        scratch=[pltpu.VMEM((rows, lanes), f32), pltpu.SemaphoreType.DMA((3,))],
    )
    return pressure_next, hull_pressure


def solution(mesh):
    cells = P("gx", "gy", "blk")
    rows = P(("gx", "gy", "blk"), None)
    return jax.shard_map(
        local,
        mesh=mesh,
        in_specs=(cells, cells, cells, cells, rows, rows, rows),
        out_specs=(cells, rows),
        check_vma=False,
    )
```
